32 devices in a mesh: gx: 8 (over y, x, core), gy: 4 (over z).
Axes of the slice: x: 2, y: 2, z: 4, core: 2. Of those that a mesh axis runs over, the one named last changes fastest.
Arguments:
- fields: float32 [4, 3, 64, 8, 8, 128], P(None, None, None, 'gx', 'gy'), may hold values from -6 to 6
- velocity: float32 [2, 3, 64, 128, 8, 8], P(None, None, None, ('gx', 'gy')), may hold values from -3 to 3
Outputs:
- advanced: float32 [4, 3, 64, 8, 8, 128], P(None, None, None, 'gx', 'gy')
The draws below stay inside these ranges and needn't reach their ends.
All inputs are finite; a program needn't handle non-finite values.
Results may differ from the reference program's by a relative error of at most 0.0003.
Values sent between devices are 32-bit elements; how exact they have to be, the bound alone decides.
A program may use at most 64 MiB of HBM per device.

```python
import jax
import jax.numpy as jnp
import numpy as np
from jax import lax

K = 4
NODES = 64
EZ = 128
STEPS = 2
NXE = 8
NYE = 8


def shard_levels(own_key, shape, split, least, top_value):
    def one(dim, blocks):
        draws = jax.random.uniform(jax.random.fold_in(jax.random.fold_in(own_key, 6), dim), (blocks,), jnp.float32, least / len(split), top_value / len(split))
        return jnp.repeat(jnp.exp(draws), shape[dim] // blocks).reshape((-1,) + (1,) * (len(shape) - dim - 1))

    factor_of = one(*split[0])
    for cut in split[1:]:
        factor_of = factor_of * one(*cut)
    return factor_of


def centred(rng, shape, deviation, bound, shards=(), dtype=jnp.bfloat16):
    entries = jax.random.normal(rng, shape, jnp.float32) * deviation
    if len(shards) > 0:
        entries = shard_levels(rng, shape, shards, -0.22, 0.18) * entries
    return jnp.clip(entries, min=-bound, max=bound).astype(dtype)


def setup_inputs(seed: int = 0) -> dict:
    key_of = jax.random.split(jax.random.key(seed), 3)
    fields = centred(key_of[0], (K, 3, NODES, NXE, NYE, EZ), 1.0, 6.0, ((3, 8), (4, 4)), jnp.float32)
    velocity = centred(key_of[1], (STEPS, 3, NODES, EZ, NXE, NYE), 0.5, 3.0, ((3, 32),), jnp.float32)
    return {"fields": fields, "velocity": velocity}


STEP_SIZE = 0.025
FLUX_COEF = 3.0
PENALTY = 3.0

def derivative_table():
    points = np.array([-1.0, -1.0 / np.sqrt(5.0), 1.0 / np.sqrt(5.0), 1.0])
    weights_bary = np.ones(4)
    for first in range(4):
        for second in range(4):
            if first != second:
                weights_bary[first] = weights_bary[first] / (points[first] - points[second])
    table = np.zeros((4, 4))
    for first in range(4):
        for second in range(4):
            if first != second:
                table[first, second] = weights_bary[second] / weights_bary[first] / (points[first] - points[second])
        table[first, first] = -np.sum(table[first])
    return jnp.asarray(table.astype(np.float32))

def along(table, block, direction):
    forms = ['pa,kabcxyz->kpbcxyz', 'pb,kabcxyz->kapcxyz', 'pc,kabcxyz->kabpxyz']
    return jnp.einsum(forms[direction], table, block, precision=lax.Precision.HIGHEST)

def cross_speed(speed, field):
    return jnp.stack([speed[1] * field[:, 2] - speed[2] * field[:, 1], speed[2] * field[:, 0] - speed[0] * field[:, 2], speed[0] * field[:, 1] - speed[1] * field[:, 0]], axis=1)

def normal_cross(direction, jump):
    zeros = jnp.zeros_like(jump[:, 0])
    if direction == 0:
        parts = [zeros, -jump[:, 2], jump[:, 1]]
    elif direction == 1:
        parts = [jump[:, 2], zeros, -jump[:, 0]]
    else:
        parts = [-jump[:, 1], jump[:, 0], zeros]
    return jnp.stack(parts, axis=1)

def tendency(field, speed, borders):
    table = derivative_table()
    elec = cross_speed(speed, field)
    result = jnp.stack([along(table, elec[:, 2], 1) - along(table, elec[:, 1], 2), along(table, elec[:, 0], 2) - along(table, elec[:, 2], 0), along(table, elec[:, 1], 0) - along(table, elec[:, 0], 1)], axis=1)
    packed = jnp.concatenate([elec, field], axis=1)
    for direction in range(3):
        node_dim = 2 + direction
        elem_dim = 4 + direction
        lower = lax.index_in_dim(packed, 0, node_dim, keepdims=False)
        upper = lax.index_in_dim(packed, 3, node_dim, keepdims=False)
        recv_low, recv_high = borders(direction, lower, upper)
        count = lower.shape[elem_dim]
        outer_high = jnp.concatenate([lax.slice_in_dim(lower, 1, count, axis=elem_dim), recv_high], axis=elem_dim)
        outer_low = jnp.concatenate([recv_low, lax.slice_in_dim(upper, 0, count - 1, axis=elem_dim)], axis=elem_dim)
        jump_high = outer_high - upper
        jump_low = outer_low - lower
        term_high = FLUX_COEF * normal_cross(direction, jump_high[:, :3]) + PENALTY * jump_high[:, 3:]
        term_low = -FLUX_COEF * normal_cross(direction, jump_low[:, :3]) + PENALTY * jump_low[:, 3:]
        high_index = (slice(None),) * node_dim + (3,)
        low_index = (slice(None),) * node_dim + (0,)
        result = result.at[high_index].add(term_high)
        result = result.at[low_index].add(term_low)
    return result

def advance(field, speed, borders):
    first = tendency(field, speed, borders)
    middle = field + STEP_SIZE * first
    second = tendency(middle, speed, borders)
    return field + 0.5 * STEP_SIZE * (first + second)

def zero_borders(direction, lower, upper):
    empty = jnp.zeros_like(lax.slice_in_dim(lower, 0, 1, axis=4 + direction))
    return (empty, empty)

def reference(fields, velocity):
    speeds = jnp.transpose(velocity, (0, 1, 2, 4, 5, 3)).reshape(STEPS, 3, 4, 4, 4, NXE, NYE, EZ)

    def one_field(field):
        state = field.reshape(1, 3, 4, 4, 4, NXE, NYE, EZ)
        for step in range(STEPS):
            state = advance(state, speeds[step], zero_borders)
        return state.reshape(3, NODES, NXE, NYE, EZ)
    return lax.map(one_field, fields)
```

```python
import functools

import jax
import jax.numpy as jnp
import numpy as np
from jax import lax
from jax.experimental import pallas as pl
from jax.experimental.pallas import tpu as pltpu
from jax.sharding import PartitionSpec as P

STEP_SIZE = 0.025
PENALTY = 3.0
MESH = pl.DeviceIdType.MESH


def derivative_table():
    points = np.array([-1.0, -1.0 / np.sqrt(5.0), 1.0 / np.sqrt(5.0), 1.0])
    weights_bary = np.ones(4)
    for first in range(4):
        for second in range(4):
            if first != second:
                weights_bary[first] = weights_bary[first] / (points[first] - points[second])
    table = np.zeros((4, 4))
    for first in range(4):
        for second in range(4):
            if first != second:
                table[first, second] = (
                    weights_bary[second] / weights_bary[first] / (points[first] - points[second])
                )
    return [[float(np.float32(table[p, q])) for q in range(4)] for p in range(4)]


TABLE = derivative_table()


def combine(p, parts):
    total = None
    for q in range(4):
        if q != p:
            term = TABLE[p][q] * parts[q]
            total = term if total is None else total + term
    return total


def d2(plane):
    parts = [plane[q : q + 1] for q in range(4)]
    return jnp.concatenate([combine(p, parts) for p in range(4)], axis=0)


def d3(plane):
    parts = [plane[:, q : q + 1] for q in range(4)]
    return jnp.concatenate([combine(p, parts) for p in range(4)], axis=1)


def load(ref, comp, a):
    return ref[comp, 128 * a : 128 * (a + 1), :].reshape(4, 4, 8, 128)


def store(ref, comp, a, value):
    ref[comp, 128 * a : 128 * (a + 1), :] = value.reshape(128, 128)


def turn(value, shift, axis):
    shape = value.shape
    rows = value.reshape(-1, 128)
    if axis == 1:
        return pltpu.roll(rows, shift, axis=1).reshape(shape)
    grouped = value.reshape(-1, 8, 128)
    return pltpu.roll(grouped, 4, axis=1).reshape(shape)


def kernel(
    count_x,
    count_y,
    fields_ref,
    speed_ref,
    out_ref,
    send_v,
    recv_v,
    layers,
    speeds,
    state,
    middle,
    half,
    elec,
    send_x,
    recv_x,
    send_y,
    recv_y,
    sem_vs,
    sem_vr,
    sem_xs,
    sem_xr,
    sem_ys,
    sem_yr,
):
    gx = lax.axis_index("gx")
    gy = lax.axis_index("gy")
    devices = count_x * count_y
    me = gx * count_y + gy
    krylov = fields_ref.shape[0]
    phases, _, slab, wide_x, wide_y, _ = speed_ref.shape

    barrier = pltpu.get_barrier_semaphore()

    def partner(i):
        other = lax.rem(me + i, devices)
        return other, (lax.div(other, count_y), lax.rem(other, count_y))

    def greet(i, carry):
        _, where = partner(i)
        pl.semaphore_signal(barrier, inc=1, device_id=where, device_id_type=MESH)
        return carry

    lax.fori_loop(1, devices, greet, 0)

    lane8 = lax.broadcasted_iota(jnp.int32, (wide_y, 128), 1)

    def pack_phase(s):
        def pack(x, carry):
            for c in range(3):
                for z in range(slab):
                    tile = speed_ref[s, c, z, x]
                    wide = jnp.concatenate([tile, tile], axis=1)
                    wide = jnp.where(lane8 < 64, wide, pltpu.roll(wide, wide_y - 1, axis=0))
                    for g in range(count_y):
                        send_v[s, x * count_y + g, c, z : z + 1, :] = wide[2 * g : 2 * g + 1]
            return carry

        lax.fori_loop(0, count_x, pack, 0)

    def speed_copy(s, other, where):
        return pltpu.make_async_remote_copy(
            src_ref=send_v.at[s, other],
            dst_ref=recv_v.at[s, me],
            send_sem=sem_vs.at[s, other],
            recv_sem=sem_vr.at[s, me],
            device_id=where,
            device_id_type=MESH,
        )

    def send_phase(s):
        def send(i, carry):
            other, where = partner(i)
            speed_copy(s, other, where).start()
            return carry

        lax.fori_loop(1, devices, send, 0)
        pltpu.make_async_copy(send_v.at[s, me], recv_v.at[s, me], sem_vr.at[s, me]).start()

    def finish_phase(s):
        def take(src, carry):
            pltpu.make_async_copy(recv_v.at[s, src], recv_v.at[s, src], sem_vr.at[s, src]).wait()
            return carry

        lax.fori_loop(0, devices, take, 0)
        for c in range(3):
            for src in range(devices):
                layers[c, slab * src : slab * (src + 1), :] = recv_v[s, src, c]
            turned = layers[c].T
            for y in range(2):
                for i in range(8):
                    rows = turned[64 * y + 8 * i : 64 * y + 8 * (i + 1)]
                    for k in range(4):
                        speeds[s, c, pl.ds(64 * i + 4 * y + k, 8, stride=8), :] = rows

    def drain_phase(s):
        def drain(i, carry):
            other, where = partner(i)
            speed_copy(s, other, where).wait_send()
            return carry

        lax.fori_loop(1, devices, drain, 0)

    has_low_x = gx > 0
    has_high_x = gx < count_x - 1
    has_low_y = gy > 0
    has_high_y = gy < count_y - 1

    def halo_copy(stage, axis, side):
        step = 1 if side == 0 else -1
        if axis == 0:
            where = (gx + step, gy)
            src, dst, ss, sr = send_x, recv_x, sem_xs, sem_xr
        else:
            where = (gx, gy + step)
            src, dst, ss, sr = send_y, recv_y, sem_ys, sem_yr
        return pltpu.make_async_remote_copy(
            src_ref=src.at[stage, side],
            dst_ref=dst.at[stage, side],
            send_sem=ss.at[stage, side],
            recv_sem=sr.at[stage, side],
            device_id=where,
            device_id_type=MESH,
        )

    halos = [
        (0, 0, has_high_x, has_low_x),
        (0, 1, has_low_x, has_high_x),
        (1, 0, has_high_y, has_low_y),
        (1, 1, has_low_y, has_high_y),
    ]

    def halo_start(stage, axis):
        for which, side, sends, _ in halos:
            if which == axis:

                @pl.when(sends)
                def _():
                    halo_copy(stage, axis, side).start()

    def halo_wait(stage, axis):
        for which, side, _, takes in halos:
            if which == axis:

                @pl.when(takes)
                def _():
                    halo_copy(stage, axis, side).wait_recv()

    def halo_drain(stage):
        for which, side, sends, _ in halos:

            @pl.when(sends)
            def _():
                halo_copy(stage, which, side).wait_send()

    row = lax.broadcasted_iota(jnp.int32, (1, 1, 8, 128), 2)
    lane = lax.broadcasted_iota(jnp.int32, (1, 1, 8, 128), 3)

    def cross_plane(field, s, a):
        b = [load(field, c, a) for c in range(3)]
        u = [load(speeds.at[s], c, a) for c in range(3)]
        e = [u[1] * b[2] - u[2] * b[1], u[2] * b[0] - u[0] * b[2], u[0] * b[1] - u[1] * b[0]]
        for c in range(3):
            store(elec, c, a, e[c])
        return b, e

    def begin(field, s, stage):
        b, e = cross_plane(field, s, 0)
        low = [b[0], b[1] - e[2], b[2] + e[1]]
        for c in range(3):
            send_x[stage, 1, c] = low[c].reshape(128, 128)
        b, e = cross_plane(field, s, 3)
        high = [b[0], b[1] + e[2], b[2] - e[1]]
        for c in range(3):
            send_x[stage, 0, c] = high[c].reshape(128, 128)
        halo_start(stage, 0)
        for a in (1, 2):
            cross_plane(field, s, a)
        for a in range(4):
            b = [load(field, c, a) for c in range(3)]
            e = [load(elec, c, a) for c in range(3)]
            low = [b[0][0:1] + e[2][0:1], b[1][0:1], b[2][0:1] - e[0][0:1]]
            high = [b[0][3:4] - e[2][3:4], b[1][3:4], b[2][3:4] + e[0][3:4]]
            for c in range(3):
                first = jnp.where(row < 4, low[c][:, 0:2], turn(low[c][:, 2:4], 4, 0))
                second = jnp.where(row < 4, turn(high[c][:, 0:2], 4, 0), high[c][:, 2:4])
                send_y[stage, 1, c, 16 * a : 16 * (a + 1), :] = first.reshape(16, 128)
                send_y[stage, 0, c, 16 * a : 16 * (a + 1), :] = second.reshape(16, 128)
        halo_start(stage, 1)

    def volume(field, a):
        b = [load(field, c, a) for c in range(3)]
        e = [load(elec, c, a) for c in range(3)]
        r = [
            d2(e[2]) - d3(e[1]),
            d3(e[0]) - combine(a, [load(elec, 2, q) for q in range(4)]),
            combine(a, [load(elec, 1, q) for q in range(4)]) - d2(e[0]),
        ]
        low2 = [b[0] - e[1], b[1] + e[0], b[2]]
        high2 = [b[0] + e[1], b[1] - e[0], b[2]]
        low1 = [b[0] + e[2], b[1], b[2] - e[0]]
        high1 = [b[0] - e[2], b[1], b[2] + e[0]]
        for c in range(3):
            from_below = jnp.where(lane > 0, turn(high2[c][:, 3:4], 1, 1), 0.0)
            from_above = jnp.where(lane < 127, turn(low2[c][:, 0:1], 127, 1), 0.0)
            gap = jnp.zeros((4, 2, 8, 128), jnp.float32)
            jump = jnp.concatenate(
                [from_below - b[c][:, 0:1], gap, from_above - b[c][:, 3:4]], axis=1
            )
            from_below = jnp.where(row >= 4, turn(high1[c][3:4], 4, 0), 0.0)
            from_above = jnp.where(row < 4, turn(low1[c][0:1], 4, 0), 0.0)
            gap = jnp.zeros((2, 4, 8, 128), jnp.float32)
            jump = jump + jnp.concatenate(
                [from_below - b[c][0:1], gap, from_above - b[c][3:4]], axis=0
            )
            if a in (0, 3):
                jump = jump - b[c]
            r[c] = r[c] + PENALTY * jump
        return b, r

    def add_halo(stage, targets):
        halo_wait(stage, 0)
        for c in range(3):
            for side, a in ((0, 0), (1, 3)):
                arrived = recv_x[stage, side, c].reshape(4, 4, 8, 128)
                for ref, scale in targets:
                    store(ref, c, a, load(ref, c, a) + (scale * PENALTY) * arrived)
        halo_wait(stage, 1)
        for c in range(3):
            for a in range(4):
                for side, b in ((0, 0), (1, 3)):
                    got = recv_y[stage, side, c, 16 * a : 16 * (a + 1), :].reshape(1, 2, 8, 128)
                    back = turn(got, 4, 0)
                    if side == 0:
                        arrived = jnp.concatenate([got, back], axis=1)
                        arrived = jnp.where(row < 4, arrived, 0.0)
                    else:
                        arrived = jnp.concatenate([back, got], axis=1)
                        arrived = jnp.where(row >= 4, arrived, 0.0)
                    at = 128 * a + 32 * b
                    arrived = arrived.reshape(32, 128)
                    for ref, scale in targets:
                        ref[c, at : at + 32, :] = (
                            ref[c, at : at + 32, :] + (scale * PENALTY) * arrived
                        )

    for which, side, _, takes in halos:

        @pl.when(jnp.logical_not(takes))
        def _():
            buffer = recv_x if which == 0 else recv_y
            for stage in range(2 * phases):
                for c in range(3):
                    buffer[stage, side, c] = jnp.zeros(buffer.shape[3:], jnp.float32)

    pack_phase(0)
    pl.semaphore_wait(barrier, devices - 1)
    send_phase(0)
    for s in range(1, phases):
        pack_phase(s)

    for k in range(krylov):
        for c in range(3):
            for j in range(16):
                state[c, pl.ds(32 * j + k, 8, stride=4), :] = fields_ref[
                    k, c, 8 * j : 8 * (j + 1), :
                ]

    for s in range(phases):
        finish_phase(s)
        stage = 2 * s
        begin(state, s, stage)
        if s + 1 < phases:
            send_phase(s + 1)
        for a in range(4):
            b, r = volume(state, a)
            for c in range(3):
                store(middle, c, a, b[c] + STEP_SIZE * r[c])
                store(half, c, a, b[c] + (0.5 * STEP_SIZE) * r[c])
        add_halo(stage, [(middle, STEP_SIZE), (half, 0.5 * STEP_SIZE)])
        begin(middle, s, stage + 1)
        for a in range(4):
            _, r = volume(middle, a)
            for c in range(3):
                store(state, c, a, load(half, c, a) + (0.5 * STEP_SIZE) * r[c])
        add_halo(stage + 1, [(state, 0.5 * STEP_SIZE)])

    for k in range(krylov):
        for c in range(3):
            for j in range(16):
                out_ref[k, c, 8 * j : 8 * (j + 1), :] = state[
                    c, pl.ds(32 * j + k, 8, stride=4), :
                ]

    for s in range(phases):
        drain_phase(s)
    for stage in range(2 * phases):
        halo_drain(stage)


def shards(count_x, count_y, fields, velocity):
    krylov, comps, nodes, elem_x, elem_y, depth = fields.shape
    phases, _, _, slab, wide_x, wide_y = velocity.shape
    devices = count_x * count_y
    stages = 2 * phases
    f32 = jnp.float32
    rows = nodes * elem_x * elem_y
    lines = krylov * rows
    body = functools.partial(kernel, count_x, count_y)
    vmem = pl.BlockSpec(memory_space=pltpu.VMEM)
    out = pl.pallas_call(
        body,
        out_shape=jax.ShapeDtypeStruct((krylov, comps, rows, depth), f32),
        in_specs=[vmem, vmem],
        out_specs=vmem,
        scratch_shapes=[
            pltpu.VMEM((phases, devices, comps, slab, 128), f32),
            pltpu.VMEM((phases, devices, comps, slab, 128), f32),
            pltpu.VMEM((comps, depth, 128), f32),
            pltpu.VMEM((phases, comps, lines, depth), f32),
            pltpu.VMEM((comps, lines, depth), f32),
            pltpu.VMEM((comps, lines, depth), f32),
            pltpu.VMEM((comps, lines, depth), f32),
            pltpu.VMEM((comps, lines, depth), f32),
            pltpu.VMEM((stages, 2, comps, 128, depth), f32),
            pltpu.VMEM((stages, 2, comps, 128, depth), f32),
            pltpu.VMEM((stages, 2, comps, 64, depth), f32),
            pltpu.VMEM((stages, 2, comps, 64, depth), f32),
            pltpu.SemaphoreType.DMA((phases, devices)),
            pltpu.SemaphoreType.DMA((phases, devices)),
            pltpu.SemaphoreType.DMA((stages, 2)),
            pltpu.SemaphoreType.DMA((stages, 2)),
            pltpu.SemaphoreType.DMA((stages, 2)),
            pltpu.SemaphoreType.DMA((stages, 2)),
        ],
        compiler_params=pltpu.CompilerParams(
            collective_id=0, has_side_effects=True, vmem_limit_bytes=48 * 1024 * 1024
        ),
    )(
        fields.reshape(krylov, comps, rows, depth),
        jnp.transpose(velocity, (0, 1, 3, 4, 5, 2)),
    )
    return out.reshape(fields.shape)


def solution(mesh):
    return jax.shard_map(
        functools.partial(shards, mesh.shape["gx"], mesh.shape["gy"]),
        mesh=mesh,
        in_specs=(
            P(None, None, None, "gx", "gy", None),
            P(None, None, None, ("gx", "gy"), None, None),
        ),
        out_specs=P(None, None, None, "gx", "gy", None),
        check_vma=False,
    )
```

```python
import functools

import jax
import jax.numpy as jnp
import numpy as np
from jax import lax
from jax.experimental import pallas as pl
from jax.experimental.pallas import tpu as pltpu
from jax.sharding import PartitionSpec as P

STEP_SIZE = 0.025
PENALTY = 3.0
MESH = pl.DeviceIdType.MESH


def derivative_table():
    points = np.array([-1.0, -1.0 / np.sqrt(5.0), 1.0 / np.sqrt(5.0), 1.0])
    weights_bary = np.ones(4)
    for first in range(4):
        for second in range(4):
            if first != second:
                weights_bary[first] = weights_bary[first] / (points[first] - points[second])
    table = np.zeros((4, 4))
    for first in range(4):
        for second in range(4):
            if first != second:
                table[first, second] = (
                    weights_bary[second] / weights_bary[first] / (points[first] - points[second])
                )
    return [[float(np.float32(table[p, q])) for q in range(4)] for p in range(4)]


TABLE = derivative_table()


def combine(p, parts):
    total = None
    for q in range(4):
        if q != p:
            term = TABLE[p][q] * parts[q]
            total = term if total is None else total + term
    return total


def d2(plane):
    parts = [plane[q : q + 1] for q in range(4)]
    return jnp.concatenate([combine(p, parts) for p in range(4)], axis=0)


def d3(plane):
    parts = [plane[:, q : q + 1] for q in range(4)]
    return jnp.concatenate([combine(p, parts) for p in range(4)], axis=1)


def load(ref, comp, a):
    return ref[comp, 128 * a : 128 * (a + 1), :].reshape(4, 4, 8, 128)


def store(ref, comp, a, value):
    ref[comp, 128 * a : 128 * (a + 1), :] = value.reshape(128, 128)


def turn(value, shift, axis):
    shape = value.shape
    rows = value.reshape(-1, 128)
    if axis == 1:
        return pltpu.roll(rows, shift, axis=1).reshape(shape)
    grouped = value.reshape(-1, 8, 128)
    return pltpu.roll(grouped, 4, axis=1).reshape(shape)


def kernel(
    count_x,
    count_y,
    fields_any,
    speed_any,
    out_ref,
    fields_ref,
    speed_ref,
    send_v,
    recv_v,
    layers,
    speeds,
    state,
    middle,
    half,
    elec,
    send_x,
    recv_x,
    send_y,
    recv_y,
    sem_vs,
    sem_vr,
    sem_xs,
    sem_xr,
    sem_ys,
    sem_yr,
    sem_in,
):
    gx = lax.axis_index("gx")
    gy = lax.axis_index("gy")
    devices = count_x * count_y
    me = gx * count_y + gy
    krylov = fields_ref.shape[0]
    phases, _, slab, wide_x, wide_y, _ = speed_ref.shape

    loads = [
        pltpu.make_async_copy(speed_any.at[s], speed_ref.at[s], sem_in.at[s])
        for s in range(phases)
    ]
    loads.append(pltpu.make_async_copy(fields_any, fields_ref, sem_in.at[phases]))
    for item in loads:
        item.start()

    barrier = pltpu.get_barrier_semaphore()

    def partner(i):
        other = lax.rem(me + i, devices)
        return other, (lax.div(other, count_y), lax.rem(other, count_y))

    def greet(i, carry):
        _, where = partner(i)
        pl.semaphore_signal(barrier, inc=1, device_id=where, device_id_type=MESH)
        return carry

    lax.fori_loop(1, devices, greet, 0)

    lane8 = lax.broadcasted_iota(jnp.int32, (wide_y, 128), 1)

    def pack_phase(s):
        def pack(x, carry):
            for c in range(3):
                for z in range(slab):
                    tile = speed_ref[s, c, z, x]
                    wide = jnp.concatenate([tile, tile], axis=1)
                    wide = jnp.where(lane8 < 64, wide, pltpu.roll(wide, wide_y - 1, axis=0))
                    for g in range(count_y):
                        send_v[s, x * count_y + g, c, z : z + 1, :] = wide[2 * g : 2 * g + 1]
            return carry

        lax.fori_loop(0, count_x, pack, 0)

    def speed_copy(s, other, where):
        return pltpu.make_async_remote_copy(
            src_ref=send_v.at[s, other],
            dst_ref=recv_v.at[s, me],
            send_sem=sem_vs.at[s, other],
            recv_sem=sem_vr.at[s, me],
            device_id=where,
            device_id_type=MESH,
        )

    def send_phase(s):
        def send(i, carry):
            other, where = partner(i)
            speed_copy(s, other, where).start()
            return carry

        lax.fori_loop(1, devices, send, 0)
        pltpu.make_async_copy(send_v.at[s, me], recv_v.at[s, me], sem_vr.at[s, me]).start()

    def finish_phase(s):
        def take(src, carry):
            pltpu.make_async_copy(recv_v.at[s, src], recv_v.at[s, src], sem_vr.at[s, src]).wait()
            return carry

        lax.fori_loop(0, devices, take, 0)
        for c in range(3):
            for src in range(devices):
                layers[c, slab * src : slab * (src + 1), :] = recv_v[s, src, c]
            turned = layers[c].T
            for y in range(2):
                for i in range(8):
                    rows = turned[64 * y + 8 * i : 64 * y + 8 * (i + 1)]
                    for k in range(4):
                        speeds[s, c, pl.ds(64 * i + 4 * y + k, 8, stride=8), :] = rows

    def drain_phase(s):
        def drain(i, carry):
            other, where = partner(i)
            speed_copy(s, other, where).wait_send()
            return carry

        lax.fori_loop(1, devices, drain, 0)

    has_low_x = gx > 0
    has_high_x = gx < count_x - 1
    has_low_y = gy > 0
    has_high_y = gy < count_y - 1

    def halo_copy(stage, axis, side):
        step = 1 if side == 0 else -1
        if axis == 0:
            where = (gx + step, gy)
            src, dst, ss, sr = send_x, recv_x, sem_xs, sem_xr
        else:
            where = (gx, gy + step)
            src, dst, ss, sr = send_y, recv_y, sem_ys, sem_yr
        return pltpu.make_async_remote_copy(
            src_ref=src.at[stage, side],
            dst_ref=dst.at[stage, side],
            send_sem=ss.at[stage, side],
            recv_sem=sr.at[stage, side],
            device_id=where,
            device_id_type=MESH,
        )

    halos = [
        (0, 0, has_high_x, has_low_x),
        (0, 1, has_low_x, has_high_x),
        (1, 0, has_high_y, has_low_y),
        (1, 1, has_low_y, has_high_y),
    ]

    def halo_start(stage, axis, sides=(0, 1)):
        for which, side, sends, _ in halos:
            if which == axis and side in sides:

                @pl.when(sends)
                def _():
                    halo_copy(stage, axis, side).start()

    def halo_wait(stage, axis):
        for which, side, _, takes in halos:
            if which == axis:

                @pl.when(takes)
                def _():
                    halo_copy(stage, axis, side).wait_recv()

    def halo_drain(stage):
        for which, side, sends, _ in halos:

            @pl.when(sends)
            def _():
                halo_copy(stage, which, side).wait_send()

    row = lax.broadcasted_iota(jnp.int32, (1, 1, 8, 128), 2)
    lane = lax.broadcasted_iota(jnp.int32, (1, 1, 8, 128), 3)

    def cross_plane(field, s, a):
        b = [load(field, c, a) for c in range(3)]
        u = [load(speeds.at[s], c, a) for c in range(3)]
        e = [u[1] * b[2] - u[2] * b[1], u[2] * b[0] - u[0] * b[2], u[0] * b[1] - u[1] * b[0]]
        for c in range(3):
            store(elec, c, a, e[c])
        return b, e

    def begin(field, s, stage):
        b, e = cross_plane(field, s, 0)
        low = [b[0], b[1] - e[2], b[2] + e[1]]
        for c in range(3):
            send_x[stage, 1, c] = low[c].reshape(128, 128)
        halo_start(stage, 0, (1,))
        b, e = cross_plane(field, s, 3)
        high = [b[0], b[1] + e[2], b[2] - e[1]]
        for c in range(3):
            send_x[stage, 0, c] = high[c].reshape(128, 128)
        halo_start(stage, 0, (0,))
        for a in (1, 2):
            cross_plane(field, s, a)
        for a in range(4):
            b = [load(field, c, a) for c in range(3)]
            e = [load(elec, c, a) for c in range(3)]
            low = [b[0][0:1] + e[2][0:1], b[1][0:1], b[2][0:1] - e[0][0:1]]
            high = [b[0][3:4] - e[2][3:4], b[1][3:4], b[2][3:4] + e[0][3:4]]
            for c in range(3):
                first = jnp.where(row < 4, low[c][:, 0:2], turn(low[c][:, 2:4], 4, 0))
                second = jnp.where(row < 4, turn(high[c][:, 0:2], 4, 0), high[c][:, 2:4])
                send_y[stage, 1, c, 16 * a : 16 * (a + 1), :] = first.reshape(16, 128)
                send_y[stage, 0, c, 16 * a : 16 * (a + 1), :] = second.reshape(16, 128)
        halo_start(stage, 1)

    def volume(field, a):
        b = [load(field, c, a) for c in range(3)]
        e = [load(elec, c, a) for c in range(3)]
        r = [
            d2(e[2]) - d3(e[1]),
            d3(e[0]) - combine(a, [load(elec, 2, q) for q in range(4)]),
            combine(a, [load(elec, 1, q) for q in range(4)]) - d2(e[0]),
        ]
        low2 = [b[0] - e[1], b[1] + e[0], b[2]]
        high2 = [b[0] + e[1], b[1] - e[0], b[2]]
        low1 = [b[0] + e[2], b[1], b[2] - e[0]]
        high1 = [b[0] - e[2], b[1], b[2] + e[0]]
        for c in range(3):
            from_below = jnp.where(lane > 0, turn(high2[c][:, 3:4], 1, 1), 0.0)
            from_above = jnp.where(lane < 127, turn(low2[c][:, 0:1], 127, 1), 0.0)
            gap = jnp.zeros((4, 2, 8, 128), jnp.float32)
            jump = jnp.concatenate(
                [from_below - b[c][:, 0:1], gap, from_above - b[c][:, 3:4]], axis=1
            )
            from_below = jnp.where(row >= 4, turn(high1[c][3:4], 4, 0), 0.0)
            from_above = jnp.where(row < 4, turn(low1[c][0:1], 4, 0), 0.0)
            gap = jnp.zeros((2, 4, 8, 128), jnp.float32)
            jump = jump + jnp.concatenate(
                [from_below - b[c][0:1], gap, from_above - b[c][3:4]], axis=0
            )
            if a in (0, 3):
                jump = jump - b[c]
            r[c] = r[c] + PENALTY * jump
        return b, r

    def add_halo(stage, targets):
        halo_wait(stage, 0)
        for c in range(3):
            for side, a in ((0, 0), (1, 3)):
                arrived = recv_x[stage, side, c].reshape(4, 4, 8, 128)
                for ref, scale in targets:
                    store(ref, c, a, load(ref, c, a) + (scale * PENALTY) * arrived)
        halo_wait(stage, 1)
        for c in range(3):
            for a in range(4):
                for side, b in ((0, 0), (1, 3)):
                    got = recv_y[stage, side, c, 16 * a : 16 * (a + 1), :].reshape(1, 2, 8, 128)
                    back = turn(got, 4, 0)
                    if side == 0:
                        arrived = jnp.concatenate([got, back], axis=1)
                        arrived = jnp.where(row < 4, arrived, 0.0)
                    else:
                        arrived = jnp.concatenate([back, got], axis=1)
                        arrived = jnp.where(row >= 4, arrived, 0.0)
                    at = 128 * a + 32 * b
                    arrived = arrived.reshape(32, 128)
                    for ref, scale in targets:
                        ref[c, at : at + 32, :] = (
                            ref[c, at : at + 32, :] + (scale * PENALTY) * arrived
                        )

    for which, side, _, takes in halos:

        @pl.when(jnp.logical_not(takes))
        def _():
            buffer = recv_x if which == 0 else recv_y
            for stage in range(2 * phases):
                for c in range(3):
                    buffer[stage, side, c] = jnp.zeros(buffer.shape[3:], jnp.float32)

    loads[0].wait()
    pack_phase(0)
    pl.semaphore_wait(barrier, devices - 1)
    send_phase(0)
    for s in range(1, phases):
        loads[s].wait()
        pack_phase(s)
    loads[phases].wait()

    for k in range(krylov):
        for c in range(3):
            for j in range(16):
                state[c, pl.ds(32 * j + k, 8, stride=4), :] = fields_ref[
                    k, c, 8 * j : 8 * (j + 1), :
                ]

    finish_phase(0)
    for s in range(phases):
        stage = 2 * s
        begin(state, s, stage)
        if s + 1 < phases:
            send_phase(s + 1)
        for a in range(4):
            b, r = volume(state, a)
            for c in range(3):
                store(middle, c, a, b[c] + STEP_SIZE * r[c])
                store(half, c, a, b[c] + (0.5 * STEP_SIZE) * r[c])
        add_halo(stage, [(middle, STEP_SIZE), (half, 0.5 * STEP_SIZE)])
        begin(middle, s, stage + 1)
        for a in range(4):
            _, r = volume(middle, a)
            for c in range(3):
                store(state, c, a, load(half, c, a) + (0.5 * STEP_SIZE) * r[c])
        if s + 1 < phases:
            finish_phase(s + 1)
        add_halo(stage + 1, [(state, 0.5 * STEP_SIZE)])

    for k in range(krylov):
        for c in range(3):
            for j in range(16):
                out_ref[k, c, 8 * j : 8 * (j + 1), :] = state[
                    c, pl.ds(32 * j + k, 8, stride=4), :
                ]

    for s in range(phases):
        drain_phase(s)
    for stage in range(2 * phases):
        halo_drain(stage)


def shards(count_x, count_y, fields, velocity):
    krylov, comps, nodes, elem_x, elem_y, depth = fields.shape
    phases, _, _, slab, wide_x, wide_y = velocity.shape
    devices = count_x * count_y
    stages = 2 * phases
    f32 = jnp.float32
    rows = nodes * elem_x * elem_y
    lines = krylov * rows
    body = functools.partial(kernel, count_x, count_y)
    vmem = pl.BlockSpec(memory_space=pltpu.VMEM)
    out = pl.pallas_call(
        body,
        out_shape=jax.ShapeDtypeStruct((krylov, comps, rows, depth), f32),
        in_specs=[pl.BlockSpec(memory_space=pl.ANY)] * 2,
        out_specs=vmem,
        scratch_shapes=[
            pltpu.VMEM((krylov, comps, rows, depth), f32),
            pltpu.VMEM((phases, comps, slab, wide_x, wide_y, nodes), f32),
            pltpu.VMEM((phases, devices, comps, slab, 128), f32),
            pltpu.VMEM((phases, devices, comps, slab, 128), f32),
            pltpu.VMEM((comps, depth, 128), f32),
            pltpu.VMEM((phases, comps, lines, depth), f32),
            pltpu.VMEM((comps, lines, depth), f32),
            pltpu.VMEM((comps, lines, depth), f32),
            pltpu.VMEM((comps, lines, depth), f32),
            pltpu.VMEM((comps, lines, depth), f32),
            pltpu.VMEM((stages, 2, comps, 128, depth), f32),
            pltpu.VMEM((stages, 2, comps, 128, depth), f32),
            pltpu.VMEM((stages, 2, comps, 64, depth), f32),
            pltpu.VMEM((stages, 2, comps, 64, depth), f32),
            pltpu.SemaphoreType.DMA((phases, devices)),
            pltpu.SemaphoreType.DMA((phases, devices)),
            pltpu.SemaphoreType.DMA((stages, 2)),
            pltpu.SemaphoreType.DMA((stages, 2)),
            pltpu.SemaphoreType.DMA((stages, 2)),
            pltpu.SemaphoreType.DMA((stages, 2)),
            pltpu.SemaphoreType.DMA((phases + 1,)),
        ],
        compiler_params=pltpu.CompilerParams(
            collective_id=0, has_side_effects=True, vmem_limit_bytes=59392 * 1024
        ),
    )(
        fields.reshape(krylov, comps, rows, depth),
        jnp.transpose(velocity, (0, 1, 3, 4, 5, 2)),
    )
    return out.reshape(fields.shape)


def solution(mesh):
    return jax.shard_map(
        functools.partial(shards, mesh.shape["gx"], mesh.shape["gy"]),
        mesh=mesh,
        in_specs=(
            P(None, None, None, "gx", "gy", None),
            P(None, None, None, ("gx", "gy"), None, None),
        ),
        out_specs=P(None, None, None, "gx", "gy", None),
        check_vma=False,
    )
```

```python
import functools

import jax
import jax.numpy as jnp
import numpy as np
from jax import lax
from jax.experimental import pallas as pl
from jax.experimental.pallas import tpu as pltpu
from jax.sharding import PartitionSpec as P

STEP_SIZE = 0.025
PENALTY = 3.0
MESH = pl.DeviceIdType.MESH


def derivative_table():
    points = np.array([-1.0, -1.0 / np.sqrt(5.0), 1.0 / np.sqrt(5.0), 1.0])
    weights_bary = np.ones(4)
    for first in range(4):
        for second in range(4):
            if first != second:
                weights_bary[first] = weights_bary[first] / (points[first] - points[second])
    table = np.zeros((4, 4))
    for first in range(4):
        for second in range(4):
            if first != second:
                table[first, second] = (
                    weights_bary[second] / weights_bary[first] / (points[first] - points[second])
                )
    return [[float(np.float32(table[p, q])) for q in range(4)] for p in range(4)]


TABLE = derivative_table()


def combine(p, parts):
    total = None
    for q in range(4):
        if q != p:
            term = TABLE[p][q] * parts[q]
            total = term if total is None else total + term
    return total


def d2(plane):
    parts = [plane[q : q + 1] for q in range(4)]
    return jnp.concatenate([combine(p, parts) for p in range(4)], axis=0)


def d3(plane):
    parts = [plane[:, q : q + 1] for q in range(4)]
    return jnp.concatenate([combine(p, parts) for p in range(4)], axis=1)


def load(ref, comp, a):
    return ref[comp, 128 * a : 128 * (a + 1), :].reshape(4, 4, 8, 128)


def store(ref, comp, a, value):
    ref[comp, 128 * a : 128 * (a + 1), :] = value.reshape(128, 128)


def turn(value, shift, axis):
    shape = value.shape
    rows = value.reshape(-1, 128)
    if axis == 1:
        return pltpu.roll(rows, shift, axis=1).reshape(shape)
    grouped = value.reshape(-1, 8, 128)
    return pltpu.roll(grouped, 4, axis=1).reshape(shape)


def kernel(
    count_x,
    count_y,
    fields_any,
    speed_any,
    out_ref,
    fields_ref,
    speed_ref,
    send_v,
    recv_v,
    layers,
    speeds,
    state,
    middle,
    elec,
    send_x,
    recv_x,
    send_y,
    recv_y,
    sem_vs,
    sem_vr,
    sem_xs,
    sem_xr,
    sem_ys,
    sem_yr,
    sem_in,
):
    gx = lax.axis_index("gx")
    gy = lax.axis_index("gy")
    devices = count_x * count_y
    me = gx * count_y + gy
    krylov = fields_ref.shape[0]
    phases, _, slab, wide_x, wide_y, _ = speed_ref.shape

    loads = [
        pltpu.make_async_copy(speed_any.at[s], speed_ref.at[s], sem_in.at[s])
        for s in range(phases)
    ]
    loads.append(pltpu.make_async_copy(fields_any, fields_ref, sem_in.at[phases]))
    for item in loads:
        item.start()

    barrier = pltpu.get_barrier_semaphore()

    def partner(i):
        other = lax.rem(me + i, devices)
        return other, (lax.div(other, count_y), lax.rem(other, count_y))

    def greet(i, carry):
        _, where = partner(i)
        pl.semaphore_signal(barrier, inc=1, device_id=where, device_id_type=MESH)
        return carry

    lax.fori_loop(1, devices, greet, 0)

    lane8 = lax.broadcasted_iota(jnp.int32, (wide_y, 128), 1)

    def pack_phase(s):
        def pack(x, carry):
            for c in range(3):
                for z in range(slab):
                    tile = speed_ref[s, c, z, x]
                    wide = jnp.concatenate([tile, tile], axis=1)
                    wide = jnp.where(lane8 < 64, wide, pltpu.roll(wide, wide_y - 1, axis=0))
                    for g in range(count_y):
                        send_v[s, x * count_y + g, c, z : z + 1, :] = wide[2 * g : 2 * g + 1]
            return carry

        lax.fori_loop(0, count_x, pack, 0)

    def speed_copy(s, other, where):
        return pltpu.make_async_remote_copy(
            src_ref=send_v.at[s, other],
            dst_ref=recv_v.at[s, me],
            send_sem=sem_vs.at[s, other],
            recv_sem=sem_vr.at[s, me],
            device_id=where,
            device_id_type=MESH,
        )

    def send_phase(s):
        def send(i, carry):
            other, where = partner(i)
            speed_copy(s, other, where).start()
            return carry

        lax.fori_loop(1, devices, send, 0)
        pltpu.make_async_copy(send_v.at[s, me], recv_v.at[s, me], sem_vr.at[s, me]).start()

    def finish_phase(s):
        def take(src, carry):
            pltpu.make_async_copy(recv_v.at[s, src], recv_v.at[s, src], sem_vr.at[s, src]).wait()
            return carry

        lax.fori_loop(0, devices, take, 0)
        for c in range(3):
            for src in range(devices):
                layers[c, slab * src : slab * (src + 1), :] = recv_v[s, src, c]
            turned = layers[c].T
            for y in range(2):
                for i in range(8):
                    rows = turned[64 * y + 8 * i : 64 * y + 8 * (i + 1)]
                    for k in range(4):
                        speeds[s, c, pl.ds(64 * i + 4 * y + k, 8, stride=8), :] = rows

    def drain_phase(s):
        def drain(i, carry):
            other, where = partner(i)
            speed_copy(s, other, where).wait_send()
            return carry

        lax.fori_loop(1, devices, drain, 0)

    has_low_x = gx > 0
    has_high_x = gx < count_x - 1
    has_low_y = gy > 0
    has_high_y = gy < count_y - 1

    def halo_copy(stage, axis, side, part):
        step = 1 if side == 0 else -1
        if axis == 0:
            where = (gx + step, gy)
            src, dst, ss, sr = send_x, recv_x, sem_xs, sem_xr
        else:
            where = (gx, gy + step)
            src, dst, ss, sr = send_y, recv_y, sem_ys, sem_yr
        return pltpu.make_async_remote_copy(
            src_ref=src.at[stage, side, part],
            dst_ref=dst.at[stage, side, part],
            send_sem=ss.at[stage, side, part],
            recv_sem=sr.at[stage, side, part],
            device_id=where,
            device_id_type=MESH,
        )

    sends = [[has_high_x, has_low_x], [has_high_y, has_low_y]]
    takes = [[has_low_x, has_high_x], [has_low_y, has_high_y]]

    def halo_start(stage, axis, side, part):
        @pl.when(sends[axis][side])
        def _():
            halo_copy(stage, axis, side, part).start()

    def halo_wait(stage, axis, side, part):
        @pl.when(takes[axis][side])
        def _():
            halo_copy(stage, axis, side, part).wait_recv()

    def halo_drain(stage):
        for axis in range(2):
            for side in range(2):

                @pl.when(sends[axis][side])
                def _():
                    for part in range(2):
                        halo_copy(stage, axis, side, part).wait_send()

    row = lax.broadcasted_iota(jnp.int32, (1, 1, 8, 128), 2)
    lane = lax.broadcasted_iota(jnp.int32, (1, 1, 8, 128), 3)

    row3 = lax.broadcasted_iota(jnp.int32, (1, 8, 128), 1)

    def block(a, b):
        return slice(128 * a + 32 * b, 128 * a + 32 * (b + 1))

    def cross_block(field, s, a, b):
        at = block(a, b)
        f = [field[c, at, :].reshape(4, 8, 128) for c in range(3)]
        u = [speeds[s, c, at, :].reshape(4, 8, 128) for c in range(3)]
        e = [u[1] * f[2] - u[2] * f[1], u[2] * f[0] - u[0] * f[2], u[0] * f[1] - u[1] * f[0]]
        for c in range(3):
            elec[c, at, :] = e[c].reshape(32, 128)
        return f, e

    def pack_x(stage, a, b, f, e):
        if a == 0:
            face = [f[0], f[1] - e[2], f[2] + e[1]]
        else:
            face = [f[0], f[1] + e[2], f[2] - e[1]]
        part, slot = (0, b - 1) if b in (1, 2) else (1, b // 3)
        for c in range(3):
            send_x[stage, 1 - a // 3, part, c, 32 * slot : 32 * (slot + 1), :] = face[c].reshape(
                32, 128
            )

    def pack_y(stage, a, b, f, e):
        if b == 0:
            face = [f[0] + e[2], f[1], f[2] - e[0]]
        else:
            face = [f[0] - e[2], f[1], f[2] + e[0]]
        part, slot = (0, a - 1) if a in (1, 2) else (1, a // 3)
        for c in range(3):
            if b == 0:
                both = jnp.where(row3 < 4, face[c][0:2], turn(face[c][2:4], 4, 0))
            else:
                both = jnp.where(row3 < 4, turn(face[c][0:2], 4, 0), face[c][2:4])
            send_y[stage, 1 - b // 3, part, c, 16 * slot : 16 * (slot + 1), :] = both.reshape(
                16, 128
            )

    def arrived_x(stage, a, b):
        part, slot = (0, b - 1) if b in (1, 2) else (1, b // 3)
        return [
            recv_x[stage, a // 3, part, c, 32 * slot : 32 * (slot + 1), :] for c in range(3)
        ]

    def arrived_y(stage, a, b):
        part, slot = (0, a - 1) if a in (1, 2) else (1, a // 3)
        found = []
        for c in range(3):
            got = recv_y[stage, b // 3, part, c, 16 * slot : 16 * (slot + 1), :]
            got = got.reshape(2, 8, 128)
            back = turn(got, 4, 0)
            if b == 0:
                full = jnp.where(row3 < 4, jnp.concatenate([got, back], axis=0), 0.0)
            else:
                full = jnp.where(row3 >= 4, jnp.concatenate([back, got], axis=0), 0.0)
            found.append(full.reshape(32, 128))
        return found

    def add_block(target, a, b, found, scale):
        at = block(a, b)
        for c in range(3):
            target[c, at, :] = target[c, at, :] + (scale * PENALTY) * found[c]

    def rims(target, s, stage, scale, arrive, onward):
        for a in (0, 3):
            if arrive:
                halo_wait(stage, 0, a // 3, 0)
            for b in (1, 2):
                if arrive:
                    add_block(target, a, b, arrived_x(stage, a, b), scale)
                if onward:
                    f, e = cross_block(target, s, a, b)
                    pack_x(stage + 1, a, b, f, e)
            if onward:
                halo_start(stage + 1, 0, 1 - a // 3, 0)
        for b in (0, 3):
            if arrive:
                halo_wait(stage, 1, b // 3, 0)
            for a in (1, 2):
                if arrive:
                    add_block(target, a, b, arrived_y(stage, a, b), scale)
                if onward:
                    f, e = cross_block(target, s, a, b)
                    pack_y(stage + 1, a, b, f, e)
            if onward:
                halo_start(stage + 1, 1, 1 - b // 3, 0)
        if arrive:
            for axis in range(2):
                for side in range(2):
                    halo_wait(stage, axis, side, 1)
        for a in (0, 3):
            for b in (0, 3):
                if arrive:
                    fx = arrived_x(stage, a, b)
                    fy = arrived_y(stage, a, b)
                    add_block(target, a, b, [fx[c] + fy[c] for c in range(3)], scale)
                if onward:
                    f, e = cross_block(target, s, a, b)
                    pack_x(stage + 1, a, b, f, e)
                    pack_y(stage + 1, a, b, f, e)
            if onward:
                halo_start(stage + 1, 0, 1 - a // 3, 1)
        if onward:
            for side in range(2):
                halo_start(stage + 1, 1, side, 1)

    def inner(field, s):
        for a in (1, 2):
            for b in (1, 2):
                cross_block(field, s, a, b)

    def volume(field, a):
        b = [load(field, c, a) for c in range(3)]
        e = [load(elec, c, a) for c in range(3)]
        r = [
            d2(e[2]) - d3(e[1]),
            d3(e[0]) - combine(a, [load(elec, 2, q) for q in range(4)]),
            combine(a, [load(elec, 1, q) for q in range(4)]) - d2(e[0]),
        ]
        low2 = [b[0] - e[1], b[1] + e[0], b[2]]
        high2 = [b[0] + e[1], b[1] - e[0], b[2]]
        low1 = [b[0] + e[2], b[1], b[2] - e[0]]
        high1 = [b[0] - e[2], b[1], b[2] + e[0]]
        for c in range(3):
            from_below = jnp.where(lane > 0, turn(high2[c][:, 3:4], 1, 1), 0.0)
            from_above = jnp.where(lane < 127, turn(low2[c][:, 0:1], 127, 1), 0.0)
            gap = jnp.zeros((4, 2, 8, 128), jnp.float32)
            jump = jnp.concatenate(
                [from_below - b[c][:, 0:1], gap, from_above - b[c][:, 3:4]], axis=1
            )
            from_below = jnp.where(row >= 4, turn(high1[c][3:4], 4, 0), 0.0)
            from_above = jnp.where(row < 4, turn(low1[c][0:1], 4, 0), 0.0)
            gap = jnp.zeros((2, 4, 8, 128), jnp.float32)
            jump = jump + jnp.concatenate(
                [from_below - b[c][0:1], gap, from_above - b[c][3:4]], axis=0
            )
            if a in (0, 3):
                jump = jump - b[c]
            r[c] = r[c] + PENALTY * jump
        return b, r

    for axis, buffer in ((0, recv_x), (1, recv_y)):
        for side in range(2):

            @pl.when(jnp.logical_not(takes[axis][side]))
            def _():
                for stage in range(2 * phases):
                    for part in range(2):
                        for c in range(3):
                            buffer[stage, side, part, c] = jnp.zeros(buffer.shape[4:], jnp.float32)

    loads[0].wait()
    pack_phase(0)
    pl.semaphore_wait(barrier, devices - 1)
    send_phase(0)
    for s in range(1, phases):
        loads[s].wait()
        pack_phase(s)
    loads[phases].wait()

    for k in range(krylov):
        for c in range(3):
            for j in range(16):
                state[c, pl.ds(32 * j + k, 8, stride=4), :] = fields_ref[
                    k, c, 8 * j : 8 * (j + 1), :
                ]

    finish_phase(0)
    rims(state, 0, -1, 0.0, False, True)
    for s in range(phases):
        stage = 2 * s
        last = s + 1 == phases
        inner(state, s)
        if not last:
            send_phase(s + 1)
        for a in range(4):
            b, r = volume(state, a)
            for c in range(3):
                store(middle, c, a, b[c] + STEP_SIZE * r[c])
        rims(middle, s, stage, STEP_SIZE, True, True)
        inner(middle, s)
        for a in range(4):
            b, r = volume(middle, a)
            for c in range(3):
                mean = 0.5 * (load(state, c, a) + b[c])
                store(state, c, a, mean + (0.5 * STEP_SIZE) * r[c])
        if not last:
            finish_phase(s + 1)
        rims(state, s + 1, stage + 1, 0.5 * STEP_SIZE, True, not last)

    for k in range(krylov):
        for c in range(3):
            for j in range(16):
                out_ref[k, c, 8 * j : 8 * (j + 1), :] = state[
                    c, pl.ds(32 * j + k, 8, stride=4), :
                ]

    for s in range(phases):
        drain_phase(s)
    for stage in range(2 * phases):
        halo_drain(stage)


def shards(count_x, count_y, fields, velocity):
    krylov, comps, nodes, elem_x, elem_y, depth = fields.shape
    phases, _, _, slab, wide_x, wide_y = velocity.shape
    devices = count_x * count_y
    stages = 2 * phases
    f32 = jnp.float32
    rows = nodes * elem_x * elem_y
    lines = krylov * rows
    body = functools.partial(kernel, count_x, count_y)
    vmem = pl.BlockSpec(memory_space=pltpu.VMEM)
    out = pl.pallas_call(
        body,
        out_shape=jax.ShapeDtypeStruct((krylov, comps, rows, depth), f32),
        in_specs=[pl.BlockSpec(memory_space=pl.ANY)] * 2,
        out_specs=vmem,
        scratch_shapes=[
            pltpu.VMEM((krylov, comps, rows, depth), f32),
            pltpu.VMEM((phases, comps, slab, wide_x, wide_y, nodes), f32),
            pltpu.VMEM((phases, devices, comps, slab, 128), f32),
            pltpu.VMEM((phases, devices, comps, slab, 128), f32),
            pltpu.VMEM((comps, depth, 128), f32),
            pltpu.VMEM((phases, comps, lines, depth), f32),
            pltpu.VMEM((comps, lines, depth), f32),
            pltpu.VMEM((comps, lines, depth), f32),
            pltpu.VMEM((comps, lines, depth), f32),
            pltpu.VMEM((stages, 2, 2, comps, 64, depth), f32),
            pltpu.VMEM((stages, 2, 2, comps, 64, depth), f32),
            pltpu.VMEM((stages, 2, 2, comps, 32, depth), f32),
            pltpu.VMEM((stages, 2, 2, comps, 32, depth), f32),
            pltpu.SemaphoreType.DMA((phases, devices)),
            pltpu.SemaphoreType.DMA((phases, devices)),
            pltpu.SemaphoreType.DMA((stages, 2, 2)),
            pltpu.SemaphoreType.DMA((stages, 2, 2)),
            pltpu.SemaphoreType.DMA((stages, 2, 2)),
            pltpu.SemaphoreType.DMA((stages, 2, 2)),
            pltpu.SemaphoreType.DMA((phases + 1,)),
        ],
        compiler_params=pltpu.CompilerParams(
            collective_id=0, has_side_effects=True, vmem_limit_bytes=58048 * 1024
        ),
    )(
        fields.reshape(krylov, comps, rows, depth),
        jnp.transpose(velocity, (0, 1, 3, 4, 5, 2)),
    )
    return out.reshape(fields.shape)


def solution(mesh):
    return jax.shard_map(
        functools.partial(shards, mesh.shape["gx"], mesh.shape["gy"]),
        mesh=mesh,
        in_specs=(
            P(None, None, None, "gx", "gy", None),
            P(None, None, None, ("gx", "gy"), None, None),
        ),
        out_specs=P(None, None, None, "gx", "gy", None),
        check_vma=False,
    )
```

```python
import functools

import jax
import jax.numpy as jnp
import numpy as np
from jax import lax
from jax.experimental import pallas as pl
from jax.experimental.pallas import tpu as pltpu
from jax.sharding import PartitionSpec as P

STEP_SIZE = 0.025
PENALTY = 3.0
MESH = pl.DeviceIdType.MESH


def derivative_table():
    points = np.array([-1.0, -1.0 / np.sqrt(5.0), 1.0 / np.sqrt(5.0), 1.0])
    weights_bary = np.ones(4)
    for first in range(4):
        for second in range(4):
            if first != second:
                weights_bary[first] = weights_bary[first] / (points[first] - points[second])
    table = np.zeros((4, 4))
    for first in range(4):
        for second in range(4):
            if first != second:
                table[first, second] = (
                    weights_bary[second] / weights_bary[first] / (points[first] - points[second])
                )
    return [[float(np.float32(table[p, q])) for q in range(4)] for p in range(4)]


TABLE = derivative_table()


def combine(p, parts):
    total = None
    for q in range(4):
        if q != p:
            term = TABLE[p][q] * parts[q]
            total = term if total is None else total + term
    return total


def d2(plane):
    parts = [plane[q : q + 1] for q in range(4)]
    return jnp.concatenate([combine(p, parts) for p in range(4)], axis=0)


def d3(plane):
    parts = [plane[:, q : q + 1] for q in range(4)]
    return jnp.concatenate([combine(p, parts) for p in range(4)], axis=1)


def load(ref, comp, a):
    return ref[comp, 128 * a : 128 * (a + 1), :].reshape(4, 4, 8, 128)


def store(ref, comp, a, value):
    ref[comp, 128 * a : 128 * (a + 1), :] = value.reshape(128, 128)


def turn(value, shift, axis):
    shape = value.shape
    rows = value.reshape(-1, 128)
    if axis == 1:
        return pltpu.roll(rows, shift, axis=1).reshape(shape)
    grouped = value.reshape(-1, 8, 128)
    return pltpu.roll(grouped, 4, axis=1).reshape(shape)


def kernel(
    count_x,
    count_y,
    fields_any,
    speed_any,
    out_ref,
    fields_ref,
    speed_ref,
    send_v,
    recv_v,
    layers,
    turned,
    speeds,
    state,
    middle,
    elec,
    send_x,
    recv_x,
    send_y,
    recv_y,
    sem_vs,
    sem_vr,
    sem_xs,
    sem_xr,
    sem_ys,
    sem_yr,
    sem_in,
):
    gx = lax.axis_index("gx")
    gy = lax.axis_index("gy")
    devices = count_x * count_y
    me = gx * count_y + gy
    krylov = fields_ref.shape[0]
    phases, _, slab, wide_x, wide_y, _ = speed_ref.shape

    loads = [
        pltpu.make_async_copy(speed_any.at[s], speed_ref.at[s], sem_in.at[s])
        for s in range(phases)
    ]
    loads.append(pltpu.make_async_copy(fields_any, fields_ref, sem_in.at[phases]))
    for item in loads:
        item.start()

    barrier = pltpu.get_barrier_semaphore()

    def partner(i):
        other = lax.rem(me + i, devices)
        return other, (lax.div(other, count_y), lax.rem(other, count_y))

    def greet(i, carry):
        _, where = partner(i)
        pl.semaphore_signal(barrier, inc=1, device_id=where, device_id_type=MESH)
        return carry

    lax.fori_loop(1, devices, greet, 0)

    lane8 = lax.broadcasted_iota(jnp.int32, (wide_y, 128), 1)

    def pack_column(s, x):
        for c in range(3):
            for z in range(slab):
                tile = speed_ref[s, c, z, x]
                wide = jnp.concatenate([tile, tile], axis=1)
                wide = jnp.where(lane8 < 64, wide, pltpu.roll(wide, wide_y - 1, axis=0))
                for g in range(count_y):
                    send_v[s, x * count_y + g, c, z : z + 1, :] = wide[2 * g : 2 * g + 1]

    def pack_phase(s):
        def pack(x, carry):
            pack_column(s, x)
            return carry

        lax.fori_loop(0, count_x, pack, 0)

    def speed_copy(s, other, where):
        return pltpu.make_async_remote_copy(
            src_ref=send_v.at[s, other],
            dst_ref=recv_v.at[s, me],
            send_sem=sem_vs.at[s, other],
            recv_sem=sem_vr.at[s, me],
            device_id=where,
            device_id_type=MESH,
        )

    def send_phase(s):
        def send(i, carry):
            other, where = partner(i)
            speed_copy(s, other, where).start()
            return carry

        lax.fori_loop(1, devices, send, 0)
        pltpu.make_async_copy(send_v.at[s, me], recv_v.at[s, me], sem_vr.at[s, me]).start()

    row2 = lax.broadcasted_iota(jnp.int32, (8, 128), 0)

    def finish_phase(s):
        def take(src, carry):
            pltpu.make_async_copy(recv_v.at[s, src], recv_v.at[s, src], sem_vr.at[s, src]).wait()
            return carry

        lax.fori_loop(0, devices, take, 0)
        for c in range(3):
            for src in range(devices):
                layers[c, slab * src : slab * (src + 1), :] = recv_v[s, src, c]
            turned[c] = layers[c].T

    def spread_block(s, a, b):
        for c in range(3):
            for i in range(4):
                node = 16 * a + 4 * b + i
                first = jnp.broadcast_to(turned[c, node : node + 1, :], (8, 128))
                second = jnp.broadcast_to(turned[c, 64 + node : 65 + node, :], (8, 128))
                speeds[c, 8 * node : 8 * (node + 1), :] = jnp.where(row2 < 4, first, second)

    def drain_phase(s):
        def drain(i, carry):
            other, where = partner(i)
            speed_copy(s, other, where).wait_send()
            return carry

        lax.fori_loop(1, devices, drain, 0)

    has_low_x = gx > 0
    has_high_x = gx < count_x - 1
    has_low_y = gy > 0
    has_high_y = gy < count_y - 1

    def halo_copy(stage, axis, side, part):
        step = 1 if side == 0 else -1
        if axis == 0:
            where = (gx + step, gy)
            src, dst, ss, sr = send_x, recv_x, sem_xs, sem_xr
        else:
            where = (gx, gy + step)
            src, dst, ss, sr = send_y, recv_y, sem_ys, sem_yr
        return pltpu.make_async_remote_copy(
            src_ref=src.at[stage, side, part],
            dst_ref=dst.at[stage, side, part],
            send_sem=ss.at[stage, side, part],
            recv_sem=sr.at[stage, side, part],
            device_id=where,
            device_id_type=MESH,
        )

    sends = [[has_high_x, has_low_x], [has_high_y, has_low_y]]
    takes = [[has_low_x, has_high_x], [has_low_y, has_high_y]]

    def halo_start(stage, axis, side, part):
        @pl.when(sends[axis][side])
        def _():
            halo_copy(stage, axis, side, part).start()

    def halo_wait(stage, axis, side, part):
        @pl.when(takes[axis][side])
        def _():
            halo_copy(stage, axis, side, part).wait_recv()

    def halo_drain(stage):
        for axis in range(2):
            for side in range(2):

                @pl.when(sends[axis][side])
                def _():
                    for part in range(2):
                        halo_copy(stage, axis, side, part).wait_send()

    row = lax.broadcasted_iota(jnp.int32, (1, 1, 8, 128), 2)
    lane = lax.broadcasted_iota(jnp.int32, (1, 1, 8, 128), 3)

    row3 = lax.broadcasted_iota(jnp.int32, (1, 8, 128), 1)

    def block(a, b):
        return slice(128 * a + 32 * b, 128 * a + 32 * (b + 1))

    def cross_block(field, fresh, a, b):
        if fresh is not None:
            spread_block(fresh, a, b)
        at = block(a, b)
        f = [field[c, at, :].reshape(4, 8, 128) for c in range(3)]
        u = [speeds[c, at, :].reshape(4, 8, 128) for c in range(3)]
        e = [u[1] * f[2] - u[2] * f[1], u[2] * f[0] - u[0] * f[2], u[0] * f[1] - u[1] * f[0]]
        for c in range(3):
            elec[c, at, :] = e[c].reshape(32, 128)
        return f, e

    def pack_x(stage, a, b, f, e):
        if a == 0:
            face = [f[0], f[1] - e[2], f[2] + e[1]]
        else:
            face = [f[0], f[1] + e[2], f[2] - e[1]]
        part, slot = (0, b - 1) if b in (1, 2) else (1, b // 3)
        for c in range(3):
            send_x[stage, 1 - a // 3, part, c, 32 * slot : 32 * (slot + 1), :] = face[c].reshape(
                32, 128
            )

    def pack_y(stage, a, b, f, e):
        if b == 0:
            face = [f[0] + e[2], f[1], f[2] - e[0]]
        else:
            face = [f[0] - e[2], f[1], f[2] + e[0]]
        part, slot = (0, a - 1) if a in (1, 2) else (1, a // 3)
        for c in range(3):
            if b == 0:
                both = jnp.where(row3 < 4, face[c][0:2], turn(face[c][2:4], 4, 0))
            else:
                both = jnp.where(row3 < 4, turn(face[c][0:2], 4, 0), face[c][2:4])
            send_y[stage, 1 - b // 3, part, c, 16 * slot : 16 * (slot + 1), :] = both.reshape(
                16, 128
            )

    def arrived_x(stage, a, b):
        part, slot = (0, b - 1) if b in (1, 2) else (1, b // 3)
        return [
            recv_x[stage, a // 3, part, c, 32 * slot : 32 * (slot + 1), :] for c in range(3)
        ]

    def arrived_y(stage, a, b):
        part, slot = (0, a - 1) if a in (1, 2) else (1, a // 3)
        found = []
        for c in range(3):
            got = recv_y[stage, b // 3, part, c, 16 * slot : 16 * (slot + 1), :]
            got = got.reshape(2, 8, 128)
            back = turn(got, 4, 0)
            if b == 0:
                full = jnp.where(row3 < 4, jnp.concatenate([got, back], axis=0), 0.0)
            else:
                full = jnp.where(row3 >= 4, jnp.concatenate([back, got], axis=0), 0.0)
            found.append(full.reshape(32, 128))
        return found

    def emit_block(a, b):
        j = 4 * a + b
        for k in range(krylov):
            for c in range(3):
                out_ref[k, c, 8 * j : 8 * (j + 1), :] = state[
                    c, pl.ds(32 * j + k, 8, stride=4), :
                ]

    def add_block(target, a, b, found, scale):
        at = block(a, b)
        for c in range(3):
            target[c, at, :] = target[c, at, :] + (scale * PENALTY) * found[c]

    def rims(target, fresh, stage, scale, arrive, onward):
        for a in (0, 3):
            if arrive:
                halo_wait(stage, 0, a // 3, 0)
            for b in (1, 2):
                if arrive:
                    add_block(target, a, b, arrived_x(stage, a, b), scale)
                if onward:
                    f, e = cross_block(target, fresh, a, b)
                    pack_x(stage + 1, a, b, f, e)
                else:
                    emit_block(a, b)
            if onward:
                halo_start(stage + 1, 0, 1 - a // 3, 0)
        for b in (0, 3):
            if arrive:
                halo_wait(stage, 1, b // 3, 0)
            for a in (1, 2):
                if arrive:
                    add_block(target, a, b, arrived_y(stage, a, b), scale)
                if onward:
                    f, e = cross_block(target, fresh, a, b)
                    pack_y(stage + 1, a, b, f, e)
                else:
                    emit_block(a, b)
            if onward:
                halo_start(stage + 1, 1, 1 - b // 3, 0)
        if arrive:
            for axis in range(2):
                for side in range(2):
                    halo_wait(stage, axis, side, 1)
        for a in (0, 3):
            for b in (0, 3):
                if arrive:
                    fx = arrived_x(stage, a, b)
                    fy = arrived_y(stage, a, b)
                    add_block(target, a, b, [fx[c] + fy[c] for c in range(3)], scale)
                if onward:
                    f, e = cross_block(target, fresh, a, b)
                    pack_x(stage + 1, a, b, f, e)
                    pack_y(stage + 1, a, b, f, e)
                else:
                    emit_block(a, b)
            if onward:
                halo_start(stage + 1, 0, 1 - a // 3, 1)
        if onward:
            for side in range(2):
                halo_start(stage + 1, 1, side, 1)

    def inner(field, fresh):
        for a in (1, 2):
            for b in (1, 2):
                cross_block(field, fresh, a, b)

    def volume(field, a):
        b = [load(field, c, a) for c in range(3)]
        e = [load(elec, c, a) for c in range(3)]
        r = [
            d2(e[2]) - d3(e[1]),
            d3(e[0]) - combine(a, [load(elec, 2, q) for q in range(4)]),
            combine(a, [load(elec, 1, q) for q in range(4)]) - d2(e[0]),
        ]
        low2 = [b[0] - e[1], b[1] + e[0], b[2]]
        high2 = [b[0] + e[1], b[1] - e[0], b[2]]
        low1 = [b[0] + e[2], b[1], b[2] - e[0]]
        high1 = [b[0] - e[2], b[1], b[2] + e[0]]
        for c in range(3):
            from_below = jnp.where(lane > 0, turn(high2[c][:, 3:4], 1, 1), 0.0)
            from_above = jnp.where(lane < 127, turn(low2[c][:, 0:1], 127, 1), 0.0)
            gap = jnp.zeros((4, 2, 8, 128), jnp.float32)
            jump = jnp.concatenate(
                [from_below - b[c][:, 0:1], gap, from_above - b[c][:, 3:4]], axis=1
            )
            from_below = jnp.where(row >= 4, turn(high1[c][3:4], 4, 0), 0.0)
            from_above = jnp.where(row < 4, turn(low1[c][0:1], 4, 0), 0.0)
            gap = jnp.zeros((2, 4, 8, 128), jnp.float32)
            jump = jump + jnp.concatenate(
                [from_below - b[c][0:1], gap, from_above - b[c][3:4]], axis=0
            )
            if a in (0, 3):
                jump = jump - b[c]
            r[c] = r[c] + PENALTY * jump
        return b, r

    for axis, buffer in ((0, recv_x), (1, recv_y)):
        for side in range(2):

            @pl.when(jnp.logical_not(takes[axis][side]))
            def _():
                for stage in range(2 * phases):
                    for part in range(2):
                        for c in range(3):
                            buffer[stage, side, part, c] = jnp.zeros(buffer.shape[4:], jnp.float32)

    loads[0].wait()
    pack_phase(0)
    pl.semaphore_wait(barrier, devices - 1)
    send_phase(0)
    for s in range(1, phases):
        loads[s].wait()
        pack_phase(s)
    loads[phases].wait()

    for k in range(krylov):
        for c in range(3):
            for j in range(16):
                state[c, pl.ds(32 * j + k, 8, stride=4), :] = fields_ref[
                    k, c, 8 * j : 8 * (j + 1), :
                ]

    finish_phase(0)
    rims(state, 0, -1, 0.0, False, True)
    for s in range(phases):
        stage = 2 * s
        last = s + 1 == phases
        inner(state, s)
        if not last:
            send_phase(s + 1)
        for a in range(4):
            b, r = volume(state, a)
            for c in range(3):
                store(middle, c, a, b[c] + STEP_SIZE * r[c])
        rims(middle, None, stage, STEP_SIZE, True, True)
        inner(middle, None)
        for a in range(4):
            b, r = volume(middle, a)
            for c in range(3):
                mean = 0.5 * (load(state, c, a) + b[c])
                store(state, c, a, mean + (0.5 * STEP_SIZE) * r[c])
        if last:
            for a in (1, 2):
                for b in (1, 2):
                    emit_block(a, b)
        else:
            finish_phase(s + 1)
        rims(state, s + 1, stage + 1, 0.5 * STEP_SIZE, True, not last)

    for s in range(phases):
        drain_phase(s)
    for stage in range(2 * phases):
        halo_drain(stage)


def shards(count_x, count_y, fields, velocity):
    krylov, comps, nodes, elem_x, elem_y, depth = fields.shape
    phases, _, _, slab, wide_x, wide_y = velocity.shape
    devices = count_x * count_y
    stages = 2 * phases
    f32 = jnp.float32
    rows = nodes * elem_x * elem_y
    lines = krylov * rows
    body = functools.partial(kernel, count_x, count_y)
    vmem = pl.BlockSpec(memory_space=pltpu.VMEM)
    out = pl.pallas_call(
        body,
        out_shape=jax.ShapeDtypeStruct((krylov, comps, rows, depth), f32),
        in_specs=[pl.BlockSpec(memory_space=pl.ANY)] * 2,
        out_specs=vmem,
        scratch_shapes=[
            pltpu.VMEM((krylov, comps, rows, depth), f32),
            pltpu.VMEM((phases, comps, slab, wide_x, wide_y, nodes), f32),
            pltpu.VMEM((phases, devices, comps, slab, 128), f32),
            pltpu.VMEM((phases, devices, comps, slab, 128), f32),
            pltpu.VMEM((comps, depth, 128), f32),
            pltpu.VMEM((comps, 128, depth), f32),
            pltpu.VMEM((comps, lines, depth), f32),
            pltpu.VMEM((comps, lines, depth), f32),
            pltpu.VMEM((comps, lines, depth), f32),
            pltpu.VMEM((comps, lines, depth), f32),
            pltpu.VMEM((stages, 2, 2, comps, 64, depth), f32),
            pltpu.VMEM((stages, 2, 2, comps, 64, depth), f32),
            pltpu.VMEM((stages, 2, 2, comps, 32, depth), f32),
            pltpu.VMEM((stages, 2, 2, comps, 32, depth), f32),
            pltpu.SemaphoreType.DMA((phases, devices)),
            pltpu.SemaphoreType.DMA((phases, devices)),
            pltpu.SemaphoreType.DMA((stages, 2, 2)),
            pltpu.SemaphoreType.DMA((stages, 2, 2)),
            pltpu.SemaphoreType.DMA((stages, 2, 2)),
            pltpu.SemaphoreType.DMA((stages, 2, 2)),
            pltpu.SemaphoreType.DMA((phases + 1,)),
        ],
        compiler_params=pltpu.CompilerParams(
            collective_id=0, has_side_effects=True, vmem_limit_bytes=55296 * 1024
        ),
    )(
        fields.reshape(krylov, comps, rows, depth),
        jnp.transpose(velocity, (0, 1, 3, 4, 5, 2)),
    )
    return out.reshape(fields.shape)


def solution(mesh):
    return jax.shard_map(
        functools.partial(shards, mesh.shape["gx"], mesh.shape["gy"]),
        mesh=mesh,
        in_specs=(
            P(None, None, None, "gx", "gy", None),
            P(None, None, None, ("gx", "gy"), None, None),
        ),
        out_specs=P(None, None, None, "gx", "gy", None),
        check_vma=False,
    )
```

```python
import functools

import jax
import jax.numpy as jnp
import numpy as np
from jax import lax
from jax.experimental import pallas as pl
from jax.experimental.pallas import tpu as pltpu
from jax.sharding import PartitionSpec as P

STEP_SIZE = 0.025
PENALTY = 3.0
MESH = pl.DeviceIdType.MESH


def derivative_table():
    points = np.array([-1.0, -1.0 / np.sqrt(5.0), 1.0 / np.sqrt(5.0), 1.0])
    weights_bary = np.ones(4)
    for first in range(4):
        for second in range(4):
            if first != second:
                weights_bary[first] = weights_bary[first] / (points[first] - points[second])
    table = np.zeros((4, 4))
    for first in range(4):
        for second in range(4):
            if first != second:
                table[first, second] = (
                    weights_bary[second] / weights_bary[first] / (points[first] - points[second])
                )
    return [[float(np.float32(table[p, q])) for q in range(4)] for p in range(4)]


TABLE = derivative_table()


def combine(p, parts):
    total = None
    for q in range(4):
        if q != p:
            term = TABLE[p][q] * parts[q]
            total = term if total is None else total + term
    return total


def d2(plane):
    parts = [plane[q : q + 1] for q in range(4)]
    return jnp.concatenate([combine(p, parts) for p in range(4)], axis=0)


def d3(plane):
    parts = [plane[:, q : q + 1] for q in range(4)]
    return jnp.concatenate([combine(p, parts) for p in range(4)], axis=1)


def load(ref, comp, a):
    return ref[comp, 128 * a : 128 * (a + 1), :].reshape(4, 4, 8, 128)


def store(ref, comp, a, value):
    ref[comp, 128 * a : 128 * (a + 1), :] = value.reshape(128, 128)


def turn(value, shift, axis):
    shape = value.shape
    rows = value.reshape(-1, 128)
    if axis == 1:
        return pltpu.roll(rows, shift, axis=1).reshape(shape)
    grouped = value.reshape(-1, 8, 128)
    return pltpu.roll(grouped, 4, axis=1).reshape(shape)


def kernel(
    count_x,
    count_y,
    fields_any,
    speed_any,
    out_ref,
    fields_ref,
    speed_ref,
    send_v,
    recv_v,
    layers,
    turned,
    speeds,
    state,
    middle,
    elec,
    send_x,
    recv_x,
    send_y,
    recv_y,
    sem_vs,
    sem_vr,
    sem_xs,
    sem_xr,
    sem_ys,
    sem_yr,
    sem_in,
    ghost_x,
    ghost_y,
    sem_gxs,
    sem_gxr,
    sem_gys,
    sem_gyr,
):
    gx = lax.axis_index("gx")
    gy = lax.axis_index("gy")
    devices = count_x * count_y
    me = gx * count_y + gy
    krylov = fields_ref.shape[0]
    phases, _, slab, wide_x, wide_y, _ = speed_ref.shape

    loads = [
        pltpu.make_async_copy(speed_any.at[s], speed_ref.at[s], sem_in.at[s])
        for s in range(phases)
    ]
    loads.append(pltpu.make_async_copy(fields_any, fields_ref, sem_in.at[phases]))
    for item in loads:
        item.start()

    barrier = pltpu.get_barrier_semaphore()

    def partner(i):
        other = lax.rem(me + i, devices)
        return other, (lax.div(other, count_y), lax.rem(other, count_y))

    def greet(i, carry):
        _, where = partner(i)
        pl.semaphore_signal(barrier, inc=1, device_id=where, device_id_type=MESH)
        return carry

    lax.fori_loop(1, devices, greet, 0)

    lane8 = lax.broadcasted_iota(jnp.int32, (wide_y, 128), 1)

    def pack_column(s, x):
        for c in range(3):
            for z in range(slab):
                tile = speed_ref[s, c, z, x]
                wide = jnp.concatenate([tile, tile], axis=1)
                wide = jnp.where(lane8 < 64, wide, pltpu.roll(wide, wide_y - 1, axis=0))
                for g in range(count_y):
                    send_v[s, x * count_y + g, c, z : z + 1, :] = wide[2 * g : 2 * g + 1]

    def pack_phase(s):
        def pack(x, carry):
            pack_column(s, x)
            return carry

        lax.fori_loop(0, count_x, pack, 0)

    def speed_copy(s, other, where):
        return pltpu.make_async_remote_copy(
            src_ref=send_v.at[s, other],
            dst_ref=recv_v.at[s, me],
            send_sem=sem_vs.at[s, other],
            recv_sem=sem_vr.at[s, me],
            device_id=where,
            device_id_type=MESH,
        )

    def send_phase(s):
        def send(i, carry):
            other, where = partner(i)
            speed_copy(s, other, where).start()
            return carry

        lax.fori_loop(1, devices, send, 0)
        pltpu.make_async_copy(send_v.at[s, me], recv_v.at[s, me], sem_vr.at[s, me]).start()

    row2 = lax.broadcasted_iota(jnp.int32, (8, 128), 0)

    def finish_phase(s):
        def take(src, carry):
            pltpu.make_async_copy(recv_v.at[s, src], recv_v.at[s, src], sem_vr.at[s, src]).wait()
            return carry

        lax.fori_loop(0, devices, take, 0)
        for c in range(3):
            for src in range(devices):
                layers[c, slab * src : slab * (src + 1), :] = recv_v[s, src, c]
            turned[s, c] = layers[c].T.reshape(2, 4, 16, 128)

    def spread_block(s, a, b):
        for c in range(3):
            for i in range(4):
                node = 16 * a + 4 * b + i
                at = 4 * b + i
                first = jnp.broadcast_to(turned[s, c, 0, a, at : at + 1, :], (8, 128))
                second = jnp.broadcast_to(turned[s, c, 1, a, at : at + 1, :], (8, 128))
                speeds[c, 8 * node : 8 * (node + 1), :] = jnp.where(row2 < 4, first, second)

    def drain_phase(s):
        def drain(i, carry):
            other, where = partner(i)
            speed_copy(s, other, where).wait_send()
            return carry

        lax.fori_loop(1, devices, drain, 0)

    has_low_x = gx > 0
    has_high_x = gx < count_x - 1
    has_low_y = gy > 0
    has_high_y = gy < count_y - 1

    def halo_copy(stage, axis, side, part):
        step = 1 if side == 0 else -1
        if axis == 0:
            where = (gx + step, gy)
            src, dst, ss, sr = send_x, recv_x, sem_xs, sem_xr
        else:
            where = (gx, gy + step)
            src, dst, ss, sr = send_y, recv_y, sem_ys, sem_yr
        return pltpu.make_async_remote_copy(
            src_ref=src.at[stage, side, part],
            dst_ref=dst.at[stage, side, part],
            send_sem=ss.at[stage, side, part],
            recv_sem=sr.at[stage, side, part],
            device_id=where,
            device_id_type=MESH,
        )

    def ghost_copy(axis, side):
        step = 1 if side == 0 else -1
        if axis == 0:
            return pltpu.make_async_remote_copy(
                src_ref=turned.at[0, :, :, 3 - 3 * side],
                dst_ref=ghost_x.at[side],
                send_sem=sem_gxs.at[side],
                recv_sem=sem_gxr.at[side],
                device_id=(gx + step, gy),
                device_id_type=MESH,
            )
        return pltpu.make_async_remote_copy(
            src_ref=turned.at[0, :, 1 - side, :, pl.ds(8 - 8 * side, 8)],
            dst_ref=ghost_y.at[side],
            send_sem=sem_gys.at[side],
            recv_sem=sem_gyr.at[side],
            device_id=(gx, gy + step),
            device_id_type=MESH,
        )

    def ghost_start():
        for axis in range(2):
            for side in range(2):

                @pl.when(sends[axis][side])
                def _():
                    ghost_copy(axis, side).start()

    def ghost_wait(axis, side):
        @pl.when(takes[axis][side])
        def _():
            ghost_copy(axis, side).wait_recv()

    def ghost_drain():
        for axis in range(2):
            for side in range(2):

                @pl.when(sends[axis][side])
                def _():
                    ghost_copy(axis, side).wait_send()

    sends = [[has_high_x, has_low_x], [has_high_y, has_low_y]]
    takes = [[has_low_x, has_high_x], [has_low_y, has_high_y]]

    def halo_start(stage, axis, side, part):
        @pl.when(sends[axis][side])
        def _():
            halo_copy(stage, axis, side, part).start()

    def halo_wait(stage, axis, side, part):
        @pl.when(takes[axis][side])
        def _():
            halo_copy(stage, axis, side, part).wait_recv()

    def halo_drain(stage):
        for axis in range(2):
            for side in range(2):

                @pl.when(sends[axis][side])
                def _():
                    for part in range(2):
                        halo_copy(stage, axis, side, part).wait_send()

    row = lax.broadcasted_iota(jnp.int32, (1, 1, 8, 128), 2)
    lane = lax.broadcasted_iota(jnp.int32, (1, 1, 8, 128), 3)

    row3 = lax.broadcasted_iota(jnp.int32, (1, 8, 128), 1)

    def block(a, b):
        return slice(128 * a + 32 * b, 128 * a + 32 * (b + 1))

    def cross_block(field, fresh, a, b):
        if fresh is not None:
            spread_block(fresh, a, b)
        at = block(a, b)
        f = [field[c, at, :].reshape(4, 8, 128) for c in range(3)]
        u = [speeds[c, at, :].reshape(4, 8, 128) for c in range(3)]
        e = cross(u, f)
        for c in range(3):
            elec[c, at, :] = e[c].reshape(32, 128)
        return f, e

    def cross(u, f):
        return [u[1] * f[2] - u[2] * f[1], u[2] * f[0] - u[0] * f[2], u[0] * f[1] - u[1] * f[0]]

    def face_x(a, f, e):
        if a == 0:
            return [f[0], f[1] - e[2], f[2] + e[1]]
        return [f[0], f[1] + e[2], f[2] - e[1]]

    def face_y(b, f, e):
        if b == 0:
            return [f[0] + e[2], f[1], f[2] - e[0]]
        return [f[0] - e[2], f[1], f[2] + e[0]]

    def pack_x(stage, a, b, face):
        part, slot = (0, b - 1) if b in (1, 2) else (1, b // 3)
        for c in range(3):
            send_x[stage, 1 - a // 3, part, c, 32 * slot : 32 * (slot + 1), :] = face[c].reshape(
                32, 128
            )

    def pack_y(stage, a, b, face):
        part, slot = (0, a - 1) if a in (1, 2) else (1, a // 3)
        for c in range(3):
            if b == 0:
                both = jnp.where(row3 < 4, face[c][0:2], turn(face[c][2:4], 4, 0))
            else:
                both = jnp.where(row3 < 4, turn(face[c][0:2], 4, 0), face[c][2:4])
            send_y[stage, 1 - b // 3, part, c, 16 * slot : 16 * (slot + 1), :] = both.reshape(
                16, 128
            )

    def arrived_x(stage, a, b):
        part, slot = (0, b - 1) if b in (1, 2) else (1, b // 3)
        side = a // 3
        f = [recv_x[stage, side, part, c, 32 * slot : 32 * (slot + 1), :] for c in range(3)]
        if stage > 0:
            return f
        f = [item.reshape(4, 8, 128) for item in f]
        u = []
        for c in range(3):
            nodes = []
            for i in range(4 * b, 4 * b + 4):
                first = jnp.broadcast_to(ghost_x[side, c, 0, i : i + 1, :], (8, 128))
                second = jnp.broadcast_to(ghost_x[side, c, 1, i : i + 1, :], (8, 128))
                nodes.append(jnp.where(row2 < 4, first, second))
            u.append(jnp.stack(nodes))
        return [item.reshape(32, 128) for item in face_x(3 - a, f, cross(u, f))]

    def arrived_y(stage, a, b):
        part, slot = (0, a - 1) if a in (1, 2) else (1, a // 3)
        side = b // 3
        f = []
        for c in range(3):
            got = recv_y[stage, side, part, c, 16 * slot : 16 * (slot + 1), :]
            got = got.reshape(2, 8, 128)
            back = turn(got, 4, 0)
            if b == 0:
                full = jnp.where(row3 < 4, jnp.concatenate([got, back], axis=0), 0.0)
            else:
                full = jnp.where(row3 >= 4, jnp.concatenate([back, got], axis=0), 0.0)
            f.append(full)
        if stage == 0:
            u = []
            for c in range(3):
                low = 4 - 4 * side
                nodes = [
                    jnp.broadcast_to(ghost_y[side, c, a, i : i + 1, :], (8, 128))
                    for i in range(low, low + 4)
                ]
                u.append(jnp.stack(nodes))
            f = face_y(3 - b, f, cross(u, f))
        return [item.reshape(32, 128) for item in f]

    def emit_block(a, b):
        j = 4 * a + b
        for k in range(krylov):
            for c in range(3):
                out_ref[k, c, 8 * j : 8 * (j + 1), :] = state[
                    c, pl.ds(32 * j + k, 8, stride=4), :
                ]

    def add_block(target, a, b, found, scale):
        at = block(a, b)
        for c in range(3):
            target[c, at, :] = target[c, at, :] + (scale * PENALTY) * found[c]

    def rims(target, fresh, stage, scale, onward):
        for a in (0, 3):
            halo_wait(stage, 0, a // 3, 0)
            if stage == 0:
                ghost_wait(0, a // 3)
            for b in (1, 2):
                add_block(target, a, b, arrived_x(stage, a, b), scale)
                if onward:
                    f, e = cross_block(target, fresh, a, b)
                    pack_x(stage + 1, a, b, face_x(a, f, e))
                else:
                    emit_block(a, b)
            if onward:
                halo_start(stage + 1, 0, 1 - a // 3, 0)
        for b in (0, 3):
            halo_wait(stage, 1, b // 3, 0)
            if stage == 0:
                ghost_wait(1, b // 3)
            for a in (1, 2):
                add_block(target, a, b, arrived_y(stage, a, b), scale)
                if onward:
                    f, e = cross_block(target, fresh, a, b)
                    pack_y(stage + 1, a, b, face_y(b, f, e))
                else:
                    emit_block(a, b)
            if onward:
                halo_start(stage + 1, 1, 1 - b // 3, 0)
        for axis in range(2):
            for side in range(2):
                halo_wait(stage, axis, side, 1)
        for a in (0, 3):
            for b in (0, 3):
                fx = arrived_x(stage, a, b)
                fy = arrived_y(stage, a, b)
                add_block(target, a, b, [fx[c] + fy[c] for c in range(3)], scale)
                if onward:
                    f, e = cross_block(target, fresh, a, b)
                    pack_x(stage + 1, a, b, face_x(a, f, e))
                    pack_y(stage + 1, a, b, face_y(b, f, e))
                else:
                    emit_block(a, b)
            if onward:
                halo_start(stage + 1, 0, 1 - a // 3, 1)
        if onward:
            for side in range(2):
                halo_start(stage + 1, 1, side, 1)

    def first_faces():
        for a in range(4):
            for b in range(4):
                f = [state[c, block(a, b), :].reshape(4, 8, 128) for c in range(3)]
                if a in (0, 3):
                    pack_x(0, a, b, f)
                if b in (0, 3):
                    pack_y(0, a, b, f)
        for axis in range(2):
            for side in range(2):
                for part in range(2):
                    halo_start(0, axis, side, part)

    def inner(field, fresh):
        for a in (1, 2):
            for b in (1, 2):
                cross_block(field, fresh, a, b)

    def volume(field, a):
        b = [load(field, c, a) for c in range(3)]
        e = [load(elec, c, a) for c in range(3)]
        r = [
            d2(e[2]) - d3(e[1]),
            d3(e[0]) - combine(a, [load(elec, 2, q) for q in range(4)]),
            combine(a, [load(elec, 1, q) for q in range(4)]) - d2(e[0]),
        ]
        low2 = [b[0] - e[1], b[1] + e[0], b[2]]
        high2 = [b[0] + e[1], b[1] - e[0], b[2]]
        low1 = [b[0] + e[2], b[1], b[2] - e[0]]
        high1 = [b[0] - e[2], b[1], b[2] + e[0]]
        for c in range(3):
            from_below = jnp.where(lane > 0, turn(high2[c][:, 3:4], 1, 1), 0.0)
            from_above = jnp.where(lane < 127, turn(low2[c][:, 0:1], 127, 1), 0.0)
            gap = jnp.zeros((4, 2, 8, 128), jnp.float32)
            jump = jnp.concatenate(
                [from_below - b[c][:, 0:1], gap, from_above - b[c][:, 3:4]], axis=1
            )
            from_below = jnp.where(row >= 4, turn(high1[c][3:4], 4, 0), 0.0)
            from_above = jnp.where(row < 4, turn(low1[c][0:1], 4, 0), 0.0)
            gap = jnp.zeros((2, 4, 8, 128), jnp.float32)
            jump = jump + jnp.concatenate(
                [from_below - b[c][0:1], gap, from_above - b[c][3:4]], axis=0
            )
            if a in (0, 3):
                jump = jump - b[c]
            r[c] = r[c] + PENALTY * jump
        return b, r

    for axis, buffer in ((0, ghost_x), (1, ghost_y)):
        for side in range(2):

            @pl.when(jnp.logical_not(takes[axis][side]))
            def _():
                buffer[side] = jnp.zeros(buffer.shape[1:], jnp.float32)

    for axis, buffer in ((0, recv_x), (1, recv_y)):
        for side in range(2):

            @pl.when(jnp.logical_not(takes[axis][side]))
            def _():
                for stage in range(2 * phases):
                    for part in range(2):
                        for c in range(3):
                            buffer[stage, side, part, c] = jnp.zeros(buffer.shape[4:], jnp.float32)

    loads[0].wait()
    pack_phase(0)
    pl.semaphore_wait(barrier, devices - 1)
    send_phase(0)
    loads[phases].wait()

    for k in range(krylov):
        for c in range(3):
            for j in range(16):
                state[c, pl.ds(32 * j + k, 8, stride=4), :] = fields_ref[
                    k, c, 8 * j : 8 * (j + 1), :
                ]
    first_faces()
    for s in range(1, phases):
        loads[s].wait()
        pack_phase(s)

    finish_phase(0)
    ghost_start()
    for s in range(phases):
        stage = 2 * s
        last = s + 1 == phases
        if s == 0:
            for a in (0, 3):
                for b in range(4):
                    cross_block(state, 0, a, b)
            for a in (1, 2):
                for b in (0, 3):
                    cross_block(state, 0, a, b)
        inner(state, s)
        if not last:
            send_phase(s + 1)
        for a in range(4):
            b, r = volume(state, a)
            for c in range(3):
                store(middle, c, a, b[c] + STEP_SIZE * r[c])
        rims(middle, None, stage, STEP_SIZE, True)
        inner(middle, None)
        for a in range(4):
            b, r = volume(middle, a)
            for c in range(3):
                mean = 0.5 * (load(state, c, a) + b[c])
                store(state, c, a, mean + (0.5 * STEP_SIZE) * r[c])
        if last:
            for a in (1, 2):
                for b in (1, 2):
                    emit_block(a, b)
        else:
            finish_phase(s + 1)
        rims(state, s + 1, stage + 1, 0.5 * STEP_SIZE, not last)

    for s in range(phases):
        drain_phase(s)
    ghost_drain()
    for stage in range(2 * phases):
        halo_drain(stage)


def shards(count_x, count_y, fields, velocity):
    krylov, comps, nodes, elem_x, elem_y, depth = fields.shape
    phases, _, _, slab, wide_x, wide_y = velocity.shape
    devices = count_x * count_y
    stages = 2 * phases
    f32 = jnp.float32
    rows = nodes * elem_x * elem_y
    lines = krylov * rows
    body = functools.partial(kernel, count_x, count_y)
    vmem = pl.BlockSpec(memory_space=pltpu.VMEM)
    out = pl.pallas_call(
        body,
        out_shape=jax.ShapeDtypeStruct((krylov, comps, rows, depth), f32),
        in_specs=[pl.BlockSpec(memory_space=pl.ANY)] * 2,
        out_specs=vmem,
        scratch_shapes=[
            pltpu.VMEM((krylov, comps, rows, depth), f32),
            pltpu.VMEM((phases, comps, slab, wide_x, wide_y, nodes), f32),
            pltpu.VMEM((phases, devices, comps, slab, 128), f32),
            pltpu.VMEM((phases, devices, comps, slab, 128), f32),
            pltpu.VMEM((comps, depth, 128), f32),
            pltpu.VMEM((phases, comps, 2, 4, 16, depth), f32),
            pltpu.VMEM((comps, lines, depth), f32),
            pltpu.VMEM((comps, lines, depth), f32),
            pltpu.VMEM((comps, lines, depth), f32),
            pltpu.VMEM((comps, lines, depth), f32),
            pltpu.VMEM((stages, 2, 2, comps, 64, depth), f32),
            pltpu.VMEM((stages, 2, 2, comps, 64, depth), f32),
            pltpu.VMEM((stages, 2, 2, comps, 32, depth), f32),
            pltpu.VMEM((stages, 2, 2, comps, 32, depth), f32),
            pltpu.SemaphoreType.DMA((phases, devices)),
            pltpu.SemaphoreType.DMA((phases, devices)),
            pltpu.SemaphoreType.DMA((stages, 2, 2)),
            pltpu.SemaphoreType.DMA((stages, 2, 2)),
            pltpu.SemaphoreType.DMA((stages, 2, 2)),
            pltpu.SemaphoreType.DMA((stages, 2, 2)),
            pltpu.SemaphoreType.DMA((phases + 1,)),
            pltpu.VMEM((2, comps, 2, 16, depth), f32),
            pltpu.VMEM((2, comps, 4, 8, depth), f32),
            pltpu.SemaphoreType.DMA((2,)),
            pltpu.SemaphoreType.DMA((2,)),
            pltpu.SemaphoreType.DMA((2,)),
            pltpu.SemaphoreType.DMA((2,)),
        ],
        compiler_params=pltpu.CompilerParams(
            collective_id=0, has_side_effects=True, vmem_limit_bytes=53248 * 1024
        ),
    )(
        fields.reshape(krylov, comps, rows, depth),
        jnp.transpose(velocity, (0, 1, 3, 4, 5, 2)),
    )
    return out.reshape(fields.shape)


def solution(mesh):
    return jax.shard_map(
        functools.partial(shards, mesh.shape["gx"], mesh.shape["gy"]),
        mesh=mesh,
        in_specs=(
            P(None, None, None, "gx", "gy", None),
            P(None, None, None, ("gx", "gy"), None, None),
        ),
        out_specs=P(None, None, None, "gx", "gy", None),
        check_vma=False,
    )
```

```python
import functools

import jax
import jax.numpy as jnp
import numpy as np
from jax import lax
from jax.experimental import pallas as pl
from jax.experimental.pallas import tpu as pltpu
from jax.sharding import PartitionSpec as P

STEP_SIZE = 0.025
PENALTY = 3.0
MESH = pl.DeviceIdType.MESH


def derivative_table():
    points = np.array([-1.0, -1.0 / np.sqrt(5.0), 1.0 / np.sqrt(5.0), 1.0])
    weights_bary = np.ones(4)
    for first in range(4):
        for second in range(4):
            if first != second:
                weights_bary[first] = weights_bary[first] / (points[first] - points[second])
    table = np.zeros((4, 4))
    for first in range(4):
        for second in range(4):
            if first != second:
                table[first, second] = (
                    weights_bary[second] / weights_bary[first] / (points[first] - points[second])
                )
    return [[float(np.float32(table[p, q])) for q in range(4)] for p in range(4)]


TABLE = derivative_table()


def combine(p, parts):
    total = None
    for q in range(4):
        if q != p:
            term = TABLE[p][q] * parts[q]
            total = term if total is None else total + term
    return total


def d2(plane):
    parts = [plane[q : q + 1] for q in range(4)]
    return jnp.concatenate([combine(p, parts) for p in range(4)], axis=0)


def d3(plane):
    parts = [plane[:, q : q + 1] for q in range(4)]
    return jnp.concatenate([combine(p, parts) for p in range(4)], axis=1)


def load(ref, comp, a):
    return ref[comp, 128 * a : 128 * (a + 1), :].reshape(4, 4, 8, 128)


def store(ref, comp, a, value):
    ref[comp, 128 * a : 128 * (a + 1), :] = value.reshape(128, 128)


def turn(value, shift, axis):
    shape = value.shape
    rows = value.reshape(-1, 128)
    if axis == 1:
        return pltpu.roll(rows, shift, axis=1).reshape(shape)
    grouped = value.reshape(-1, 8, 128)
    return pltpu.roll(grouped, 4, axis=1).reshape(shape)


def kernel(
    count_x,
    count_y,
    fields_any,
    speed_any,
    out_ref,
    fields_ref,
    speed_ref,
    send_v,
    recv_v,
    layers,
    turned,
    speeds,
    state,
    middle,
    elec,
    send_x,
    recv_x,
    send_y,
    recv_y,
    sem_vs,
    sem_vr,
    sem_xs,
    sem_xr,
    sem_ys,
    sem_yr,
    sem_in,
    ghost_x,
    ghost_y,
    sem_gxs,
    sem_gxr,
    sem_gys,
    sem_gyr,
):
    gx = lax.axis_index("gx")
    gy = lax.axis_index("gy")
    devices = count_x * count_y
    me = gx * count_y + gy
    krylov = fields_ref.shape[0]
    phases, _, slab, wide_x, wide_y, _ = speed_ref.shape

    loads = [
        pltpu.make_async_copy(speed_any.at[s], speed_ref.at[s], sem_in.at[s])
        for s in range(phases)
    ]
    loads.append(pltpu.make_async_copy(fields_any, fields_ref, sem_in.at[phases]))
    for item in loads:
        item.start()

    barrier = pltpu.get_barrier_semaphore()

    def partner(i):
        other = lax.rem(me + i, devices)
        return other, (lax.div(other, count_y), lax.rem(other, count_y))

    def greet(i, carry):
        _, where = partner(i)
        pl.semaphore_signal(barrier, inc=1, device_id=where, device_id_type=MESH)
        return carry

    lax.fori_loop(1, devices, greet, 0)

    lane8 = lax.broadcasted_iota(jnp.int32, (wide_y, 128), 1)

    def pack_column(s, x):
        for c in range(3):
            for z in range(slab):
                tile = speed_ref[s, c, z, x]
                wide = jnp.concatenate([tile, tile], axis=1)
                wide = jnp.where(lane8 < 64, wide, pltpu.roll(wide, wide_y - 1, axis=0))
                for g in range(count_y):
                    send_v[s, x * count_y + g, c, z : z + 1, :] = wide[2 * g : 2 * g + 1]

    def pack_phase(s):
        def pack(x, carry):
            pack_column(s, x)
            return carry

        lax.fori_loop(0, count_x, pack, 0)

    def speed_copy(s, other, where):
        return pltpu.make_async_remote_copy(
            src_ref=send_v.at[s, other],
            dst_ref=recv_v.at[s, me],
            send_sem=sem_vs.at[s, other],
            recv_sem=sem_vr.at[s, me],
            device_id=where,
            device_id_type=MESH,
        )

    def send_phase(s):
        def send(i, carry):
            other, where = partner(i)
            speed_copy(s, other, where).start()
            return carry

        lax.fori_loop(1, devices, send, 0)
        pltpu.make_async_copy(send_v.at[s, me], recv_v.at[s, me], sem_vr.at[s, me]).start()

    row2 = lax.broadcasted_iota(jnp.int32, (8, 128), 0)

    def finish_phase(s):
        def take(src, carry):
            pltpu.make_async_copy(recv_v.at[s, src], recv_v.at[s, src], sem_vr.at[s, src]).wait()
            return carry

        lax.fori_loop(0, devices, take, 0)
        for c in range(3):
            for src in range(devices):
                layers[c, slab * src : slab * (src + 1), :] = recv_v[s, src, c]
            turned[s, c] = layers[c].T.reshape(2, 4, 16, 128)

    def spread_block(s, a, b):
        for c in range(3):
            for i in range(4):
                node = 16 * a + 4 * b + i
                at = 4 * b + i
                first = jnp.broadcast_to(turned[s, c, 0, a, at : at + 1, :], (8, 128))
                second = jnp.broadcast_to(turned[s, c, 1, a, at : at + 1, :], (8, 128))
                speeds[c, 8 * node : 8 * (node + 1), :] = jnp.where(row2 < 4, first, second)

    def drain_phase(s):
        def drain(i, carry):
            other, where = partner(i)
            speed_copy(s, other, where).wait_send()
            return carry

        lax.fori_loop(1, devices, drain, 0)

    has_low_x = gx > 0
    has_high_x = gx < count_x - 1
    has_low_y = gy > 0
    has_high_y = gy < count_y - 1

    def halo_copy(stage, axis, side, part):
        step = 1 if side == 0 else -1
        if axis == 0:
            where = (gx + step, gy)
            src, dst, ss, sr = send_x, recv_x, sem_xs, sem_xr
        else:
            where = (gx, gy + step)
            src, dst, ss, sr = send_y, recv_y, sem_ys, sem_yr
        return pltpu.make_async_remote_copy(
            src_ref=src.at[stage, side, part],
            dst_ref=dst.at[stage, side, part],
            send_sem=ss.at[stage, side, part],
            recv_sem=sr.at[stage, side, part],
            device_id=where,
            device_id_type=MESH,
        )

    def ghost_copy(axis, side):
        step = 1 if side == 0 else -1
        if axis == 0:
            return pltpu.make_async_remote_copy(
                src_ref=turned.at[0, :, :, 3 - 3 * side],
                dst_ref=ghost_x.at[side],
                send_sem=sem_gxs.at[side],
                recv_sem=sem_gxr.at[side],
                device_id=(gx + step, gy),
                device_id_type=MESH,
            )
        return pltpu.make_async_remote_copy(
            src_ref=turned.at[0, :, 1 - side, :, pl.ds(8 - 8 * side, 8)],
            dst_ref=ghost_y.at[side],
            send_sem=sem_gys.at[side],
            recv_sem=sem_gyr.at[side],
            device_id=(gx, gy + step),
            device_id_type=MESH,
        )

    def ghost_start():
        for axis in range(2):
            for side in range(2):

                @pl.when(sends[axis][side])
                def _():
                    ghost_copy(axis, side).start()

    def ghost_wait(axis, side):
        @pl.when(takes[axis][side])
        def _():
            ghost_copy(axis, side).wait_recv()

    def ghost_drain():
        for axis in range(2):
            for side in range(2):

                @pl.when(sends[axis][side])
                def _():
                    ghost_copy(axis, side).wait_send()

    sends = [[has_high_x, has_low_x], [has_high_y, has_low_y]]
    takes = [[has_low_x, has_high_x], [has_low_y, has_high_y]]

    def halo_start(stage, axis, side, part):
        @pl.when(sends[axis][side])
        def _():
            halo_copy(stage, axis, side, part).start()

    def halo_wait(stage, axis, side, part):
        @pl.when(takes[axis][side])
        def _():
            halo_copy(stage, axis, side, part).wait_recv()

    def halo_drain(stage):
        for axis in range(2):
            for side in range(2):

                @pl.when(sends[axis][side])
                def _():
                    for part in range(2):
                        halo_copy(stage, axis, side, part).wait_send()

    row = lax.broadcasted_iota(jnp.int32, (1, 1, 8, 128), 2)
    lane = lax.broadcasted_iota(jnp.int32, (1, 1, 8, 128), 3)

    row3 = lax.broadcasted_iota(jnp.int32, (1, 8, 128), 1)

    def block(a, b):
        return slice(128 * a + 32 * b, 128 * a + 32 * (b + 1))

    def cross_block(field, fresh, a, b):
        if fresh is not None:
            spread_block(fresh, a, b)
        at = block(a, b)
        f = [field[c, at, :].reshape(4, 8, 128) for c in range(3)]
        u = [speeds[c, at, :].reshape(4, 8, 128) for c in range(3)]
        e = cross(u, f)
        for c in range(3):
            elec[c, at, :] = e[c].reshape(32, 128)
        return f, e

    def cross(u, f):
        return [u[1] * f[2] - u[2] * f[1], u[2] * f[0] - u[0] * f[2], u[0] * f[1] - u[1] * f[0]]

    def face_x(a, f, e):
        if a == 0:
            return [f[0], f[1] - e[2], f[2] + e[1]]
        return [f[0], f[1] + e[2], f[2] - e[1]]

    def face_y(b, f, e):
        if b == 0:
            return [f[0] + e[2], f[1], f[2] - e[0]]
        return [f[0] - e[2], f[1], f[2] + e[0]]

    def pack_x(stage, a, b, face):
        part, slot = (0, b - 1) if b in (1, 2) else (1, b // 3)
        for c in range(3):
            send_x[stage, 1 - a // 3, part, c, 32 * slot : 32 * (slot + 1), :] = face[c].reshape(
                32, 128
            )

    def pack_y(stage, a, b, face):
        part, slot = (0, a - 1) if a in (1, 2) else (1, a // 3)
        for c in range(3):
            if b == 0:
                both = jnp.where(row3 < 4, face[c][0:2], turn(face[c][2:4], 4, 0))
            else:
                both = jnp.where(row3 < 4, turn(face[c][0:2], 4, 0), face[c][2:4])
            send_y[stage, 1 - b // 3, part, c, 16 * slot : 16 * (slot + 1), :] = both.reshape(
                16, 128
            )

    def arrived_x(stage, a, b):
        part, slot = (0, b - 1) if b in (1, 2) else (1, b // 3)
        side = a // 3
        f = [recv_x[stage, side, part, c, 32 * slot : 32 * (slot + 1), :] for c in range(3)]
        if stage > 0:
            return f
        f = [item.reshape(4, 8, 128) for item in f]
        u = []
        for c in range(3):
            nodes = []
            for i in range(4 * b, 4 * b + 4):
                first = jnp.broadcast_to(ghost_x[side, c, 0, i : i + 1, :], (8, 128))
                second = jnp.broadcast_to(ghost_x[side, c, 1, i : i + 1, :], (8, 128))
                nodes.append(jnp.where(row2 < 4, first, second))
            u.append(jnp.stack(nodes))
        return [item.reshape(32, 128) for item in face_x(3 - a, f, cross(u, f))]

    def arrived_y(stage, a, b):
        part, slot = (0, a - 1) if a in (1, 2) else (1, a // 3)
        side = b // 3
        f = []
        for c in range(3):
            got = recv_y[stage, side, part, c, 16 * slot : 16 * (slot + 1), :]
            got = got.reshape(2, 8, 128)
            back = turn(got, 4, 0)
            if b == 0:
                full = jnp.where(row3 < 4, jnp.concatenate([got, back], axis=0), 0.0)
            else:
                full = jnp.where(row3 >= 4, jnp.concatenate([back, got], axis=0), 0.0)
            f.append(full)
        if stage == 0:
            u = []
            for c in range(3):
                low = 4 - 4 * side
                nodes = [
                    jnp.broadcast_to(ghost_y[side, c, a, i : i + 1, :], (8, 128))
                    for i in range(low, low + 4)
                ]
                u.append(jnp.stack(nodes))
            f = face_y(3 - b, f, cross(u, f))
        return [item.reshape(32, 128) for item in f]

    def emit_block(a, b):
        j = 4 * a + b
        for k in range(krylov):
            for c in range(3):
                out_ref[k, c, 8 * j : 8 * (j + 1), :] = state[
                    c, pl.ds(32 * j + k, 8, stride=4), :
                ]

    def add_block(target, a, b, found, scale):
        at = block(a, b)
        for c in range(3):
            target[c, at, :] = target[c, at, :] + (scale * PENALTY) * found[c]

    def rims(target, fresh, stage, scale, onward):
        for a in (0, 3):
            halo_wait(stage, 0, a // 3, 0)
            if stage == 0:
                ghost_wait(0, a // 3)
            for b in (1, 2):
                add_block(target, a, b, arrived_x(stage, a, b), scale)
                if onward:
                    f, e = cross_block(target, fresh, a, b)
                    pack_x(stage + 1, a, b, face_x(a, f, e))
                else:
                    emit_block(a, b)
            if onward:
                halo_start(stage + 1, 0, 1 - a // 3, 0)
        for b in (0, 3):
            halo_wait(stage, 1, b // 3, 0)
            if stage == 0:
                ghost_wait(1, b // 3)
            for a in (1, 2):
                add_block(target, a, b, arrived_y(stage, a, b), scale)
                if onward:
                    f, e = cross_block(target, fresh, a, b)
                    pack_y(stage + 1, a, b, face_y(b, f, e))
                else:
                    emit_block(a, b)
            if onward:
                halo_start(stage + 1, 1, 1 - b // 3, 0)
        for axis in range(2):
            for side in range(2):
                halo_wait(stage, axis, side, 1)
        for a in (0, 3):
            for b in (0, 3):
                fx = arrived_x(stage, a, b)
                fy = arrived_y(stage, a, b)
                add_block(target, a, b, [fx[c] + fy[c] for c in range(3)], scale)
                if onward:
                    f, e = cross_block(target, fresh, a, b)
                    pack_x(stage + 1, a, b, face_x(a, f, e))
                    pack_y(stage + 1, a, b, face_y(b, f, e))
                else:
                    emit_block(a, b)
            if onward:
                halo_start(stage + 1, 0, 1 - a // 3, 1)
        if onward:
            for side in range(2):
                halo_start(stage + 1, 1, side, 1)

    def first_faces():
        for a in range(4):
            for b in range(4):
                f = [state[c, block(a, b), :].reshape(4, 8, 128) for c in range(3)]
                if a in (0, 3):
                    pack_x(0, a, b, f)
                if b in (0, 3):
                    pack_y(0, a, b, f)
        for axis in range(2):
            for side in range(2):
                for part in range(2):
                    halo_start(0, axis, side, part)

    def inner(field, fresh):
        for a in (1, 2):
            for b in (1, 2):
                cross_block(field, fresh, a, b)

    def volume(field, a):
        b = [load(field, c, a) for c in range(3)]
        e = [load(elec, c, a) for c in range(3)]
        r = [
            d2(e[2]) - d3(e[1]),
            d3(e[0]) - combine(a, [load(elec, 2, q) for q in range(4)]),
            combine(a, [load(elec, 1, q) for q in range(4)]) - d2(e[0]),
        ]
        low2 = [b[0] - e[1], b[1] + e[0], b[2]]
        high2 = [b[0] + e[1], b[1] - e[0], b[2]]
        low1 = [b[0] + e[2], b[1], b[2] - e[0]]
        high1 = [b[0] - e[2], b[1], b[2] + e[0]]
        for c in range(3):
            from_below = jnp.where(lane > 0, turn(high2[c][:, 3:4], 1, 1), 0.0)
            from_above = jnp.where(lane < 127, turn(low2[c][:, 0:1], 127, 1), 0.0)
            gap = jnp.zeros((4, 2, 8, 128), jnp.float32)
            jump = jnp.concatenate(
                [from_below - b[c][:, 0:1], gap, from_above - b[c][:, 3:4]], axis=1
            )
            from_below = jnp.where(row >= 4, turn(high1[c][3:4], 4, 0), 0.0)
            from_above = jnp.where(row < 4, turn(low1[c][0:1], 4, 0), 0.0)
            gap = jnp.zeros((2, 4, 8, 128), jnp.float32)
            jump = jump + jnp.concatenate(
                [from_below - b[c][0:1], gap, from_above - b[c][3:4]], axis=0
            )
            if a in (0, 3):
                jump = jump - b[c]
            r[c] = r[c] + PENALTY * jump
        return b, r

    for axis, buffer in ((0, ghost_x), (1, ghost_y)):
        for side in range(2):

            @pl.when(jnp.logical_not(takes[axis][side]))
            def _():
                buffer[side] = jnp.zeros(buffer.shape[1:], jnp.float32)

    for axis, buffer in ((0, recv_x), (1, recv_y)):
        for side in range(2):

            @pl.when(jnp.logical_not(takes[axis][side]))
            def _():
                for stage in range(2 * phases):
                    for part in range(2):
                        for c in range(3):
                            buffer[stage, side, part, c] = jnp.zeros(buffer.shape[4:], jnp.float32)

    loads[0].wait()
    pack_phase(0)
    pl.semaphore_wait(barrier, devices - 1)
    send_phase(0)
    loads[phases].wait()

    for k in range(krylov):
        for c in range(3):
            for j in range(16):
                state[c, pl.ds(32 * j + k, 8, stride=4), :] = fields_ref[
                    k, c, 8 * j : 8 * (j + 1), :
                ]
    first_faces()
    for s in range(1, phases):
        loads[s].wait()
        pack_phase(s)
        send_phase(s)

    finish_phase(0)
    ghost_start()
    for s in range(phases):
        stage = 2 * s
        last = s + 1 == phases
        if s == 0:
            for a in (0, 3):
                for b in range(4):
                    cross_block(state, 0, a, b)
            for a in (1, 2):
                for b in (0, 3):
                    cross_block(state, 0, a, b)
        inner(state, s)
        for a in range(4):
            b, r = volume(state, a)
            for c in range(3):
                store(middle, c, a, b[c] + STEP_SIZE * r[c])
        rims(middle, None, stage, STEP_SIZE, True)
        inner(middle, None)
        for a in range(4):
            b, r = volume(middle, a)
            for c in range(3):
                mean = 0.5 * (load(state, c, a) + b[c])
                store(state, c, a, mean + (0.5 * STEP_SIZE) * r[c])
        if last:
            for a in (1, 2):
                for b in (1, 2):
                    emit_block(a, b)
        else:
            finish_phase(s + 1)
        rims(state, s + 1, stage + 1, 0.5 * STEP_SIZE, not last)

    for s in range(phases):
        drain_phase(s)
    ghost_drain()
    for stage in range(2 * phases):
        halo_drain(stage)


def shards(count_x, count_y, fields, velocity):
    krylov, comps, nodes, elem_x, elem_y, depth = fields.shape
    phases, _, _, slab, wide_x, wide_y = velocity.shape
    devices = count_x * count_y
    stages = 2 * phases
    f32 = jnp.float32
    rows = nodes * elem_x * elem_y
    lines = krylov * rows
    body = functools.partial(kernel, count_x, count_y)
    vmem = pl.BlockSpec(memory_space=pltpu.VMEM)
    out = pl.pallas_call(
        body,
        out_shape=jax.ShapeDtypeStruct((krylov, comps, rows, depth), f32),
        in_specs=[pl.BlockSpec(memory_space=pl.ANY)] * 2,
        out_specs=vmem,
        scratch_shapes=[
            pltpu.VMEM((krylov, comps, rows, depth), f32),
            pltpu.VMEM((phases, comps, slab, wide_x, wide_y, nodes), f32),
            pltpu.VMEM((phases, devices, comps, slab, 128), f32),
            pltpu.VMEM((phases, devices, comps, slab, 128), f32),
            pltpu.VMEM((comps, depth, 128), f32),
            pltpu.VMEM((phases, comps, 2, 4, 16, depth), f32),
            pltpu.VMEM((comps, lines, depth), f32),
            pltpu.VMEM((comps, lines, depth), f32),
            pltpu.VMEM((comps, lines, depth), f32),
            pltpu.VMEM((comps, lines, depth), f32),
            pltpu.VMEM((stages, 2, 2, comps, 64, depth), f32),
            pltpu.VMEM((stages, 2, 2, comps, 64, depth), f32),
            pltpu.VMEM((stages, 2, 2, comps, 32, depth), f32),
            pltpu.VMEM((stages, 2, 2, comps, 32, depth), f32),
            pltpu.SemaphoreType.DMA((phases, devices)),
            pltpu.SemaphoreType.DMA((phases, devices)),
            pltpu.SemaphoreType.DMA((stages, 2, 2)),
            pltpu.SemaphoreType.DMA((stages, 2, 2)),
            pltpu.SemaphoreType.DMA((stages, 2, 2)),
            pltpu.SemaphoreType.DMA((stages, 2, 2)),
            pltpu.SemaphoreType.DMA((phases + 1,)),
            pltpu.VMEM((2, comps, 2, 16, depth), f32),
            pltpu.VMEM((2, comps, 4, 8, depth), f32),
            pltpu.SemaphoreType.DMA((2,)),
            pltpu.SemaphoreType.DMA((2,)),
            pltpu.SemaphoreType.DMA((2,)),
            pltpu.SemaphoreType.DMA((2,)),
        ],
        compiler_params=pltpu.CompilerParams(
            collective_id=0, has_side_effects=True, vmem_limit_bytes=54016 * 1024
        ),
    )(
        fields.reshape(krylov, comps, rows, depth),
        jnp.transpose(velocity, (0, 1, 3, 4, 5, 2)),
    )
    return out.reshape(fields.shape)


def solution(mesh):
    return jax.shard_map(
        functools.partial(shards, mesh.shape["gx"], mesh.shape["gy"]),
        mesh=mesh,
        in_specs=(
            P(None, None, None, "gx", "gy", None),
            P(None, None, None, ("gx", "gy"), None, None),
        ),
        out_specs=P(None, None, None, "gx", "gy", None),
        check_vma=False,
    )
```

```python
import functools

import jax
import jax.numpy as jnp
import numpy as np
from jax import lax
from jax.experimental import pallas as pl
from jax.experimental.pallas import tpu as pltpu
from jax.sharding import PartitionSpec as P

STEP_SIZE = 0.025
PENALTY = 3.0
MESH = pl.DeviceIdType.MESH


def derivative_table():
    points = np.array([-1.0, -1.0 / np.sqrt(5.0), 1.0 / np.sqrt(5.0), 1.0])
    weights_bary = np.ones(4)
    for first in range(4):
        for second in range(4):
            if first != second:
                weights_bary[first] = weights_bary[first] / (points[first] - points[second])
    table = np.zeros((4, 4))
    for first in range(4):
        for second in range(4):
            if first != second:
                table[first, second] = (
                    weights_bary[second] / weights_bary[first] / (points[first] - points[second])
                )
    return [[float(np.float32(table[p, q])) for q in range(4)] for p in range(4)]


TABLE = derivative_table()


def combine(p, parts):
    total = None
    for q in range(4):
        if q != p:
            term = TABLE[p][q] * parts[q]
            total = term if total is None else total + term
    return total


def d2(plane):
    parts = [plane[q : q + 1] for q in range(4)]
    return jnp.concatenate([combine(p, parts) for p in range(4)], axis=0)


def d3(plane):
    parts = [plane[:, q : q + 1] for q in range(4)]
    return jnp.concatenate([combine(p, parts) for p in range(4)], axis=1)


def load(ref, comp, a):
    return ref[comp, 128 * a : 128 * (a + 1), :].reshape(4, 4, 8, 128)


def store(ref, comp, a, value):
    ref[comp, 128 * a : 128 * (a + 1), :] = value.reshape(128, 128)


def turn(value, shift, axis):
    shape = value.shape
    rows = value.reshape(-1, 128)
    if axis == 1:
        return pltpu.roll(rows, shift, axis=1).reshape(shape)
    grouped = value.reshape(-1, 8, 128)
    return pltpu.roll(grouped, 4, axis=1).reshape(shape)


def kernel(
    count_x,
    count_y,
    fields_any,
    speed_any,
    out_ref,
    fields_ref,
    speed_ref,
    send_v,
    recv_v,
    layers,
    turned,
    speeds,
    state,
    middle,
    elec,
    send_x,
    recv_x,
    send_y,
    recv_y,
    sem_vs,
    sem_vr,
    sem_xs,
    sem_xr,
    sem_ys,
    sem_yr,
    sem_in,
    ghost_x,
    ghost_y,
    sem_gxs,
    sem_gxr,
    sem_gys,
    sem_gyr,
):
    gx = lax.axis_index("gx")
    gy = lax.axis_index("gy")
    devices = count_x * count_y
    me = gx * count_y + gy
    krylov = fields_ref.shape[0]
    phases, _, slab, wide_x, wide_y, _ = speed_ref.shape

    loads = [
        pltpu.make_async_copy(speed_any.at[s], speed_ref.at[s], sem_in.at[s])
        for s in range(phases)
    ]
    loads.append(pltpu.make_async_copy(fields_any, fields_ref, sem_in.at[phases]))
    for item in loads:
        item.start()

    barrier = pltpu.get_barrier_semaphore()

    def partner(i):
        other = lax.rem(me + i, devices)
        return other, (lax.div(other, count_y), lax.rem(other, count_y))

    def greet(i, carry):
        _, where = partner(i)
        pl.semaphore_signal(barrier, inc=1, device_id=where, device_id_type=MESH)
        return carry

    lax.fori_loop(1, devices, greet, 0)

    lane8 = lax.broadcasted_iota(jnp.int32, (wide_y, 128), 1)

    def pack_column(s, x):
        for c in range(3):
            for z in range(slab):
                tile = speed_ref[s, c, z, x]
                wide = jnp.concatenate([tile, tile], axis=1)
                wide = jnp.where(lane8 < 64, wide, pltpu.roll(wide, wide_y - 1, axis=0))
                for g in range(count_y):
                    send_v[s, x * count_y + g, c, z : z + 1, :] = wide[2 * g : 2 * g + 1]

    def pack_phase(s):
        def pack(x, carry):
            pack_column(s, x)
            return carry

        lax.fori_loop(0, count_x, pack, 0)

    def speed_copy(s, other, where):
        return pltpu.make_async_remote_copy(
            src_ref=send_v.at[s, other],
            dst_ref=recv_v.at[s, me],
            send_sem=sem_vs.at[s, other],
            recv_sem=sem_vr.at[s, me],
            device_id=where,
            device_id_type=MESH,
        )

    def send_phase(s):
        def send(i, carry):
            other, where = partner(i)
            speed_copy(s, other, where).start()
            return carry

        lax.fori_loop(1, devices, send, 0)
        pltpu.make_async_copy(send_v.at[s, me], recv_v.at[s, me], sem_vr.at[s, me]).start()

    row2 = lax.broadcasted_iota(jnp.int32, (8, 128), 0)

    def finish_phase(s):
        for src in range(devices):
            pltpu.make_async_copy(recv_v.at[s, src], recv_v.at[s, src], sem_vr.at[s, src]).wait()
            for c in range(3):
                layers[c, slab * src : slab * (src + 1), :] = recv_v[s, src, c]
        for c in range(3):
            turned[s, c] = layers[c].T.reshape(2, 4, 16, 128)

    def spread_block(s, a, b):
        for c in range(3):
            for i in range(4):
                node = 16 * a + 4 * b + i
                at = 4 * b + i
                first = jnp.broadcast_to(turned[s, c, 0, a, at : at + 1, :], (8, 128))
                second = jnp.broadcast_to(turned[s, c, 1, a, at : at + 1, :], (8, 128))
                speeds[c, 8 * node : 8 * (node + 1), :] = jnp.where(row2 < 4, first, second)

    def drain_phase(s):
        def drain(i, carry):
            other, where = partner(i)
            speed_copy(s, other, where).wait_send()
            return carry

        lax.fori_loop(1, devices, drain, 0)

    has_low_x = gx > 0
    has_high_x = gx < count_x - 1
    has_low_y = gy > 0
    has_high_y = gy < count_y - 1

    def halo_copy(stage, axis, side, part):
        step = 1 if side == 0 else -1
        if axis == 0:
            where = (gx + step, gy)
            src, dst, ss, sr = send_x, recv_x, sem_xs, sem_xr
        else:
            where = (gx, gy + step)
            src, dst, ss, sr = send_y, recv_y, sem_ys, sem_yr
        return pltpu.make_async_remote_copy(
            src_ref=src.at[stage, side, part],
            dst_ref=dst.at[stage, side, part],
            send_sem=ss.at[stage, side, part],
            recv_sem=sr.at[stage, side, part],
            device_id=where,
            device_id_type=MESH,
        )

    def ghost_copy(axis, side):
        step = 1 if side == 0 else -1
        if axis == 0:
            return pltpu.make_async_remote_copy(
                src_ref=turned.at[0, :, :, 3 - 3 * side],
                dst_ref=ghost_x.at[side],
                send_sem=sem_gxs.at[side],
                recv_sem=sem_gxr.at[side],
                device_id=(gx + step, gy),
                device_id_type=MESH,
            )
        return pltpu.make_async_remote_copy(
            src_ref=turned.at[0, :, 1 - side, :, pl.ds(8 - 8 * side, 8)],
            dst_ref=ghost_y.at[side],
            send_sem=sem_gys.at[side],
            recv_sem=sem_gyr.at[side],
            device_id=(gx, gy + step),
            device_id_type=MESH,
        )

    def ghost_start():
        for axis in range(2):
            for side in range(2):

                @pl.when(sends[axis][side])
                def _():
                    ghost_copy(axis, side).start()

    def ghost_wait(axis, side):
        @pl.when(takes[axis][side])
        def _():
            ghost_copy(axis, side).wait_recv()

    def ghost_drain():
        for axis in range(2):
            for side in range(2):

                @pl.when(sends[axis][side])
                def _():
                    ghost_copy(axis, side).wait_send()

    sends = [[has_high_x, has_low_x], [has_high_y, has_low_y]]
    takes = [[has_low_x, has_high_x], [has_low_y, has_high_y]]

    def halo_start(stage, axis, side, part):
        @pl.when(sends[axis][side])
        def _():
            halo_copy(stage, axis, side, part).start()

    def halo_wait(stage, axis, side, part):
        @pl.when(takes[axis][side])
        def _():
            halo_copy(stage, axis, side, part).wait_recv()

    def halo_drain(stage):
        for axis in range(2):
            for side in range(2):

                @pl.when(sends[axis][side])
                def _():
                    for part in range(2):
                        halo_copy(stage, axis, side, part).wait_send()

    row = lax.broadcasted_iota(jnp.int32, (1, 1, 8, 128), 2)
    lane = lax.broadcasted_iota(jnp.int32, (1, 1, 8, 128), 3)

    row3 = lax.broadcasted_iota(jnp.int32, (1, 8, 128), 1)

    def block(a, b):
        return slice(128 * a + 32 * b, 128 * a + 32 * (b + 1))

    def cross_block(field, fresh, a, b):
        if fresh is not None:
            spread_block(fresh, a, b)
        at = block(a, b)
        f = [field[c, at, :].reshape(4, 8, 128) for c in range(3)]
        u = [speeds[c, at, :].reshape(4, 8, 128) for c in range(3)]
        e = cross(u, f)
        for c in range(3):
            elec[c, at, :] = e[c].reshape(32, 128)
        return f, e

    def cross(u, f):
        return [u[1] * f[2] - u[2] * f[1], u[2] * f[0] - u[0] * f[2], u[0] * f[1] - u[1] * f[0]]

    def face_x(a, f, e):
        if a == 0:
            return [f[0], f[1] - e[2], f[2] + e[1]]
        return [f[0], f[1] + e[2], f[2] - e[1]]

    def face_y(b, f, e):
        if b == 0:
            return [f[0] + e[2], f[1], f[2] - e[0]]
        return [f[0] - e[2], f[1], f[2] + e[0]]

    def pack_x(stage, a, b, face):
        part, slot = (0, b - 1) if b in (1, 2) else (1, b // 3)
        for c in range(3):
            send_x[stage, 1 - a // 3, part, c, 32 * slot : 32 * (slot + 1), :] = face[c].reshape(
                32, 128
            )

    def pack_y(stage, a, b, face):
        part, slot = (0, a - 1) if a in (1, 2) else (1, a // 3)
        for c in range(3):
            if b == 0:
                both = jnp.where(row3 < 4, face[c][0:2], turn(face[c][2:4], 4, 0))
            else:
                both = jnp.where(row3 < 4, turn(face[c][0:2], 4, 0), face[c][2:4])
            send_y[stage, 1 - b // 3, part, c, 16 * slot : 16 * (slot + 1), :] = both.reshape(
                16, 128
            )

    def arrived_x(stage, a, b):
        part, slot = (0, b - 1) if b in (1, 2) else (1, b // 3)
        side = a // 3
        f = [recv_x[stage, side, part, c, 32 * slot : 32 * (slot + 1), :] for c in range(3)]
        if stage > 0:
            return f
        f = [item.reshape(4, 8, 128) for item in f]
        u = []
        for c in range(3):
            nodes = []
            for i in range(4 * b, 4 * b + 4):
                first = jnp.broadcast_to(ghost_x[side, c, 0, i : i + 1, :], (8, 128))
                second = jnp.broadcast_to(ghost_x[side, c, 1, i : i + 1, :], (8, 128))
                nodes.append(jnp.where(row2 < 4, first, second))
            u.append(jnp.stack(nodes))
        return [item.reshape(32, 128) for item in face_x(3 - a, f, cross(u, f))]

    def arrived_y(stage, a, b):
        part, slot = (0, a - 1) if a in (1, 2) else (1, a // 3)
        side = b // 3
        f = []
        for c in range(3):
            got = recv_y[stage, side, part, c, 16 * slot : 16 * (slot + 1), :]
            got = got.reshape(2, 8, 128)
            back = turn(got, 4, 0)
            if b == 0:
                full = jnp.where(row3 < 4, jnp.concatenate([got, back], axis=0), 0.0)
            else:
                full = jnp.where(row3 >= 4, jnp.concatenate([back, got], axis=0), 0.0)
            f.append(full)
        if stage == 0:
            u = []
            for c in range(3):
                low = 4 - 4 * side
                nodes = [
                    jnp.broadcast_to(ghost_y[side, c, a, i : i + 1, :], (8, 128))
                    for i in range(low, low + 4)
                ]
                u.append(jnp.stack(nodes))
            f = face_y(3 - b, f, cross(u, f))
        return [item.reshape(32, 128) for item in f]

    def emit_block(a, b):
        j = 4 * a + b
        for k in range(krylov):
            for c in range(3):
                out_ref[k, c, 8 * j : 8 * (j + 1), :] = state[
                    c, pl.ds(32 * j + k, 8, stride=4), :
                ]

    def add_block(target, a, b, found, scale):
        at = block(a, b)
        for c in range(3):
            target[c, at, :] = target[c, at, :] + (scale * PENALTY) * found[c]

    def rims(target, fresh, stage, scale, onward):
        for b in (0, 3):
            halo_wait(stage, 1, b // 3, 0)
            if stage == 0:
                ghost_wait(1, b // 3)
            for a in (1, 2):
                add_block(target, a, b, arrived_y(stage, a, b), scale)
                if onward:
                    f, e = cross_block(target, fresh, a, b)
                    pack_y(stage + 1, a, b, face_y(b, f, e))
                else:
                    emit_block(a, b)
            if onward:
                halo_start(stage + 1, 1, 1 - b // 3, 0)
        for a in (0, 3):
            halo_wait(stage, 0, a // 3, 0)
            if stage == 0:
                ghost_wait(0, a // 3)
            for b in (1, 2):
                add_block(target, a, b, arrived_x(stage, a, b), scale)
                if onward:
                    f, e = cross_block(target, fresh, a, b)
                    pack_x(stage + 1, a, b, face_x(a, f, e))
                else:
                    emit_block(a, b)
            if onward:
                halo_start(stage + 1, 0, 1 - a // 3, 0)
        for axis in range(2):
            for side in range(2):
                halo_wait(stage, axis, side, 1)
        for a in (0, 3):
            for b in (0, 3):
                fx = arrived_x(stage, a, b)
                fy = arrived_y(stage, a, b)
                add_block(target, a, b, [fx[c] + fy[c] for c in range(3)], scale)
                if onward:
                    f, e = cross_block(target, fresh, a, b)
                    pack_x(stage + 1, a, b, face_x(a, f, e))
                    pack_y(stage + 1, a, b, face_y(b, f, e))
                else:
                    emit_block(a, b)
            if onward:
                halo_start(stage + 1, 0, 1 - a // 3, 1)
        if onward:
            for side in range(2):
                halo_start(stage + 1, 1, side, 1)

    def first_faces():
        for a in range(4):
            for b in range(4):
                f = [state[c, block(a, b), :].reshape(4, 8, 128) for c in range(3)]
                if a in (0, 3):
                    pack_x(0, a, b, f)
                if b in (0, 3):
                    pack_y(0, a, b, f)
        for axis in range(2):
            for side in range(2):
                for part in range(2):
                    halo_start(0, axis, side, part)

    def inner(field, fresh):
        for a in (1, 2):
            for b in (1, 2):
                cross_block(field, fresh, a, b)

    def volume(field, a):
        b = [load(field, c, a) for c in range(3)]
        e = [load(elec, c, a) for c in range(3)]
        r = [
            d2(e[2]) - d3(e[1]),
            d3(e[0]) - combine(a, [load(elec, 2, q) for q in range(4)]),
            combine(a, [load(elec, 1, q) for q in range(4)]) - d2(e[0]),
        ]
        low2 = [b[0] - e[1], b[1] + e[0], b[2]]
        high2 = [b[0] + e[1], b[1] - e[0], b[2]]
        low1 = [b[0] + e[2], b[1], b[2] - e[0]]
        high1 = [b[0] - e[2], b[1], b[2] + e[0]]
        for c in range(3):
            from_below = jnp.where(lane > 0, turn(high2[c][:, 3:4], 1, 1), 0.0)
            from_above = jnp.where(lane < 127, turn(low2[c][:, 0:1], 127, 1), 0.0)
            gap = jnp.zeros((4, 2, 8, 128), jnp.float32)
            jump = jnp.concatenate(
                [from_below - b[c][:, 0:1], gap, from_above - b[c][:, 3:4]], axis=1
            )
            from_below = jnp.where(row >= 4, turn(high1[c][3:4], 4, 0), 0.0)
            from_above = jnp.where(row < 4, turn(low1[c][0:1], 4, 0), 0.0)
            gap = jnp.zeros((2, 4, 8, 128), jnp.float32)
            jump = jump + jnp.concatenate(
                [from_below - b[c][0:1], gap, from_above - b[c][3:4]], axis=0
            )
            if a in (0, 3):
                jump = jump - b[c]
            r[c] = r[c] + PENALTY * jump
        return b, r

    for axis, buffer in ((0, ghost_x), (1, ghost_y)):
        for side in range(2):

            @pl.when(jnp.logical_not(takes[axis][side]))
            def _():
                buffer[side] = jnp.zeros(buffer.shape[1:], jnp.float32)

    for axis, buffer in ((0, recv_x), (1, recv_y)):
        for side in range(2):

            @pl.when(jnp.logical_not(takes[axis][side]))
            def _():
                for stage in range(2 * phases):
                    for part in range(2):
                        for c in range(3):
                            buffer[stage, side, part, c] = jnp.zeros(buffer.shape[4:], jnp.float32)

    loads[0].wait()
    pack_phase(0)
    pl.semaphore_wait(barrier, devices - 1)
    send_phase(0)
    loads[phases].wait()

    for k in range(krylov):
        for c in range(3):
            for j in range(16):
                state[c, pl.ds(32 * j + k, 8, stride=4), :] = fields_ref[
                    k, c, 8 * j : 8 * (j + 1), :
                ]
    first_faces()
    for s in range(1, phases):
        loads[s].wait()
        pack_phase(s)
        send_phase(s)

    finish_phase(0)
    ghost_start()
    for s in range(phases):
        stage = 2 * s
        last = s + 1 == phases
        if s == 0:
            for a in (0, 3):
                for b in range(4):
                    cross_block(state, 0, a, b)
            for a in (1, 2):
                for b in (0, 3):
                    cross_block(state, 0, a, b)
        inner(state, s)
        for a in range(4):
            b, r = volume(state, a)
            for c in range(3):
                store(middle, c, a, b[c] + STEP_SIZE * r[c])
        rims(middle, None, stage, STEP_SIZE, True)
        inner(middle, None)
        for a in range(4):
            b, r = volume(middle, a)
            for c in range(3):
                mean = 0.5 * (load(state, c, a) + b[c])
                store(state, c, a, mean + (0.5 * STEP_SIZE) * r[c])
        if last:
            for a in (1, 2):
                for b in (1, 2):
                    emit_block(a, b)
        else:
            finish_phase(s + 1)
        rims(state, s + 1, stage + 1, 0.5 * STEP_SIZE, not last)

    for s in range(phases):
        drain_phase(s)
    ghost_drain()
    for stage in range(2 * phases):
        halo_drain(stage)


def shards(count_x, count_y, fields, velocity):
    krylov, comps, nodes, elem_x, elem_y, depth = fields.shape
    phases, _, _, slab, wide_x, wide_y = velocity.shape
    devices = count_x * count_y
    stages = 2 * phases
    f32 = jnp.float32
    rows = nodes * elem_x * elem_y
    lines = krylov * rows
    body = functools.partial(kernel, count_x, count_y)
    vmem = pl.BlockSpec(memory_space=pltpu.VMEM)
    out = pl.pallas_call(
        body,
        out_shape=jax.ShapeDtypeStruct((krylov, comps, rows, depth), f32),
        in_specs=[pl.BlockSpec(memory_space=pl.ANY)] * 2,
        out_specs=vmem,
        scratch_shapes=[
            pltpu.VMEM((krylov, comps, rows, depth), f32),
            pltpu.VMEM((phases, comps, slab, wide_x, wide_y, nodes), f32),
            pltpu.VMEM((phases, devices, comps, slab, 128), f32),
            pltpu.VMEM((phases, devices, comps, slab, 128), f32),
            pltpu.VMEM((comps, depth, 128), f32),
            pltpu.VMEM((phases, comps, 2, 4, 16, depth), f32),
            pltpu.VMEM((comps, lines, depth), f32),
            pltpu.VMEM((comps, lines, depth), f32),
            pltpu.VMEM((comps, lines, depth), f32),
            pltpu.VMEM((comps, lines, depth), f32),
            pltpu.VMEM((stages, 2, 2, comps, 64, depth), f32),
            pltpu.VMEM((stages, 2, 2, comps, 64, depth), f32),
            pltpu.VMEM((stages, 2, 2, comps, 32, depth), f32),
            pltpu.VMEM((stages, 2, 2, comps, 32, depth), f32),
            pltpu.SemaphoreType.DMA((phases, devices)),
            pltpu.SemaphoreType.DMA((phases, devices)),
            pltpu.SemaphoreType.DMA((stages, 2, 2)),
            pltpu.SemaphoreType.DMA((stages, 2, 2)),
            pltpu.SemaphoreType.DMA((stages, 2, 2)),
            pltpu.SemaphoreType.DMA((stages, 2, 2)),
            pltpu.SemaphoreType.DMA((phases + 1,)),
            pltpu.VMEM((2, comps, 2, 16, depth), f32),
            pltpu.VMEM((2, comps, 4, 8, depth), f32),
            pltpu.SemaphoreType.DMA((2,)),
            pltpu.SemaphoreType.DMA((2,)),
            pltpu.SemaphoreType.DMA((2,)),
            pltpu.SemaphoreType.DMA((2,)),
        ],
        compiler_params=pltpu.CompilerParams(
            collective_id=0, has_side_effects=True, vmem_limit_bytes=54016 * 1024
        ),
    )(
        fields.reshape(krylov, comps, rows, depth),
        jnp.transpose(velocity, (0, 1, 3, 4, 5, 2)),
    )
    return out.reshape(fields.shape)


def solution(mesh):
    return jax.shard_map(
        functools.partial(shards, mesh.shape["gx"], mesh.shape["gy"]),
        mesh=mesh,
        in_specs=(
            P(None, None, None, "gx", "gy", None),
            P(None, None, None, ("gx", "gy"), None, None),
        ),
        out_specs=P(None, None, None, "gx", "gy", None),
        check_vma=False,
    )
```

```python
import functools

import jax
import jax.numpy as jnp
import numpy as np
from jax import lax
from jax.experimental import pallas as pl
from jax.experimental.pallas import tpu as pltpu
from jax.sharding import PartitionSpec as P

STEP_SIZE = 0.025
PENALTY = 3.0
MESH = pl.DeviceIdType.MESH


def derivative_table():
    points = np.array([-1.0, -1.0 / np.sqrt(5.0), 1.0 / np.sqrt(5.0), 1.0])
    weights_bary = np.ones(4)
    for first in range(4):
        for second in range(4):
            if first != second:
                weights_bary[first] = weights_bary[first] / (points[first] - points[second])
    table = np.zeros((4, 4))
    for first in range(4):
        for second in range(4):
            if first != second:
                table[first, second] = (
                    weights_bary[second] / weights_bary[first] / (points[first] - points[second])
                )
    return [[float(np.float32(table[p, q])) for q in range(4)] for p in range(4)]


TABLE = derivative_table()


def combine(p, parts):
    total = None
    for q in range(4):
        if q != p:
            term = TABLE[p][q] * parts[q]
            total = term if total is None else total + term
    return total


def d2(plane):
    parts = [plane[q : q + 1] for q in range(4)]
    return jnp.concatenate([combine(p, parts) for p in range(4)], axis=0)


def d3(plane):
    parts = [plane[:, q : q + 1] for q in range(4)]
    return jnp.concatenate([combine(p, parts) for p in range(4)], axis=1)


def load(ref, comp, a):
    return ref[comp, 128 * a : 128 * (a + 1), :].reshape(4, 4, 8, 128)


def store(ref, comp, a, value):
    ref[comp, 128 * a : 128 * (a + 1), :] = value.reshape(128, 128)


def turn(value, shift, axis):
    shape = value.shape
    rows = value.reshape(-1, 128)
    if axis == 1:
        return pltpu.roll(rows, shift, axis=1).reshape(shape)
    grouped = value.reshape(-1, 8, 128)
    return pltpu.roll(grouped, 4, axis=1).reshape(shape)


def kernel(
    count_x,
    count_y,
    fields_any,
    speed_any,
    out_ref,
    fields_ref,
    speed_ref,
    send_v,
    recv_v,
    layers,
    turned,
    speeds,
    state,
    middle,
    elec,
    send_x,
    recv_x,
    send_y,
    recv_y,
    sem_vs,
    sem_vr,
    sem_xs,
    sem_xr,
    sem_ys,
    sem_yr,
    sem_in,
    ghost_x,
    ghost_y,
    sem_gxs,
    sem_gxr,
    sem_gys,
    sem_gyr,
):
    gx = lax.axis_index("gx")
    gy = lax.axis_index("gy")
    devices = count_x * count_y
    me = gx * count_y + gy
    krylov = fields_ref.shape[0]
    phases, _, slab, wide_x, wide_y, _ = speed_ref.shape

    loads = [
        pltpu.make_async_copy(speed_any.at[s], speed_ref.at[s], sem_in.at[s])
        for s in range(phases)
    ]
    loads.append(pltpu.make_async_copy(fields_any, fields_ref, sem_in.at[phases]))
    for item in loads:
        item.start()

    barrier = pltpu.get_barrier_semaphore()

    def partner(i):
        other = lax.rem(me + i, devices)
        return other, (lax.div(other, count_y), lax.rem(other, count_y))

    def greet(i, carry):
        _, where = partner(i)
        pl.semaphore_signal(barrier, inc=1, device_id=where, device_id_type=MESH)
        return carry

    lax.fori_loop(1, devices, greet, 0)

    lane8 = lax.broadcasted_iota(jnp.int32, (wide_y, 128), 1)

    def pack_column(s, x):
        for c in range(3):
            for z in range(slab):
                tile = speed_ref[s, c, z, x]
                wide = jnp.concatenate([tile, tile], axis=1)
                wide = jnp.where(lane8 < 64, wide, pltpu.roll(wide, wide_y - 1, axis=0))
                for g in range(count_y):
                    send_v[s, x * count_y + g, c, z : z + 1, :] = wide[2 * g : 2 * g + 1]

    def pack_phase(s):
        def pack(x, carry):
            pack_column(s, x)
            return carry

        lax.fori_loop(0, count_x, pack, 0)

    def speed_copy(s, other, where):
        return pltpu.make_async_remote_copy(
            src_ref=send_v.at[s, other],
            dst_ref=recv_v.at[s, me],
            send_sem=sem_vs.at[s, other],
            recv_sem=sem_vr.at[s, me],
            device_id=where,
            device_id_type=MESH,
        )

    def send_phase(s):
        def send(i, carry):
            other, where = partner(i)
            speed_copy(s, other, where).start()
            return carry

        lax.fori_loop(1, devices, send, 0)
        pltpu.make_async_copy(send_v.at[s, me], recv_v.at[s, me], sem_vr.at[s, me]).start()

    row2 = lax.broadcasted_iota(jnp.int32, (8, 128), 0)

    def finish_phase(s):
        def take(src, carry):
            pltpu.make_async_copy(recv_v.at[s, src], recv_v.at[s, src], sem_vr.at[s, src]).wait()
            return carry

        lax.fori_loop(0, devices, take, 0)
        for c in range(3):
            for src in range(devices):
                layers[c, slab * src : slab * (src + 1), :] = recv_v[s, src, c]
            turned[s, c] = layers[c].T.reshape(2, 4, 16, 128)

    def spread_block(s, a, b):
        for c in range(3):
            for i in range(4):
                node = 16 * a + 4 * b + i
                at = 4 * b + i
                first = jnp.broadcast_to(turned[s, c, 0, a, at : at + 1, :], (8, 128))
                second = jnp.broadcast_to(turned[s, c, 1, a, at : at + 1, :], (8, 128))
                speeds[c, 8 * node : 8 * (node + 1), :] = jnp.where(row2 < 4, first, second)

    def drain_phase(s):
        def drain(i, carry):
            other, where = partner(i)
            speed_copy(s, other, where).wait_send()
            return carry

        lax.fori_loop(1, devices, drain, 0)

    has_low_x = gx > 0
    has_high_x = gx < count_x - 1
    has_low_y = gy > 0
    has_high_y = gy < count_y - 1

    def halo_copy(stage, axis, side, part):
        step = 1 if side == 0 else -1
        if axis == 0:
            where = (gx + step, gy)
            src, dst, ss, sr = send_x, recv_x, sem_xs, sem_xr
        else:
            where = (gx, gy + step)
            src, dst, ss, sr = send_y, recv_y, sem_ys, sem_yr
        return pltpu.make_async_remote_copy(
            src_ref=src.at[stage, side, part],
            dst_ref=dst.at[stage, side, part],
            send_sem=ss.at[stage, side, part],
            recv_sem=sr.at[stage, side, part],
            device_id=where,
            device_id_type=MESH,
        )

    def ghost_copy(axis, side):
        step = 1 if side == 0 else -1
        if axis == 0:
            return pltpu.make_async_remote_copy(
                src_ref=turned.at[0, :, :, 3 - 3 * side],
                dst_ref=ghost_x.at[side],
                send_sem=sem_gxs.at[side],
                recv_sem=sem_gxr.at[side],
                device_id=(gx + step, gy),
                device_id_type=MESH,
            )
        return pltpu.make_async_remote_copy(
            src_ref=turned.at[0, :, 1 - side, :, pl.ds(8 - 8 * side, 8)],
            dst_ref=ghost_y.at[side],
            send_sem=sem_gys.at[side],
            recv_sem=sem_gyr.at[side],
            device_id=(gx, gy + step),
            device_id_type=MESH,
        )

    def ghost_start():
        for axis in range(2):
            for side in range(2):

                @pl.when(sends[axis][side])
                def _():
                    ghost_copy(axis, side).start()

    def ghost_wait(axis, side):
        @pl.when(takes[axis][side])
        def _():
            ghost_copy(axis, side).wait_recv()

    def ghost_drain():
        for axis in range(2):
            for side in range(2):

                @pl.when(sends[axis][side])
                def _():
                    ghost_copy(axis, side).wait_send()

    sends = [[has_high_x, has_low_x], [has_high_y, has_low_y]]
    takes = [[has_low_x, has_high_x], [has_low_y, has_high_y]]

    def halo_start(stage, axis, side, part):
        @pl.when(sends[axis][side])
        def _():
            halo_copy(stage, axis, side, part).start()

    def halo_wait(stage, axis, side, part):
        @pl.when(takes[axis][side])
        def _():
            halo_copy(stage, axis, side, part).wait_recv()

    def halo_drain(stage):
        for axis in range(2):
            for side in range(2):

                @pl.when(sends[axis][side])
                def _():
                    for part in range(2):
                        halo_copy(stage, axis, side, part).wait_send()

    row = lax.broadcasted_iota(jnp.int32, (1, 1, 8, 128), 2)
    lane = lax.broadcasted_iota(jnp.int32, (1, 1, 8, 128), 3)

    row3 = lax.broadcasted_iota(jnp.int32, (1, 8, 128), 1)

    def block(a, b):
        return slice(128 * a + 32 * b, 128 * a + 32 * (b + 1))

    def cross_block(field, fresh, a, b):
        if fresh is not None:
            spread_block(fresh, a, b)
        at = block(a, b)
        f = [field[c, at, :].reshape(4, 8, 128) for c in range(3)]
        u = [speeds[c, at, :].reshape(4, 8, 128) for c in range(3)]
        e = cross(u, f)
        for c in range(3):
            elec[c, at, :] = e[c].reshape(32, 128)
        return f, e

    def cross(u, f):
        return [u[1] * f[2] - u[2] * f[1], u[2] * f[0] - u[0] * f[2], u[0] * f[1] - u[1] * f[0]]

    def face_x(a, f, e):
        if a == 0:
            return [f[0], f[1] - e[2], f[2] + e[1]]
        return [f[0], f[1] + e[2], f[2] - e[1]]

    def face_y(b, f, e):
        if b == 0:
            return [f[0] + e[2], f[1], f[2] - e[0]]
        return [f[0] - e[2], f[1], f[2] + e[0]]

    def pack_x(stage, a, b, face):
        part, slot = (0, b - 1) if b in (1, 2) else (1, b // 3)
        for c in range(3):
            send_x[stage, 1 - a // 3, part, c, 32 * slot : 32 * (slot + 1), :] = face[c].reshape(
                32, 128
            )

    def pack_y(stage, a, b, face):
        part, slot = (0, a - 1) if a in (1, 2) else (1, a // 3)
        for c in range(3):
            if b == 0:
                both = jnp.where(row3 < 4, face[c][0:2], turn(face[c][2:4], 4, 0))
            else:
                both = jnp.where(row3 < 4, turn(face[c][0:2], 4, 0), face[c][2:4])
            send_y[stage, 1 - b // 3, part, c, 16 * slot : 16 * (slot + 1), :] = both.reshape(
                16, 128
            )

    def arrived_x(stage, a, b):
        part, slot = (0, b - 1) if b in (1, 2) else (1, b // 3)
        side = a // 3
        f = [recv_x[stage, side, part, c, 32 * slot : 32 * (slot + 1), :] for c in range(3)]
        if stage > 0:
            return f
        f = [item.reshape(4, 8, 128) for item in f]
        u = []
        for c in range(3):
            nodes = []
            for i in range(4 * b, 4 * b + 4):
                first = jnp.broadcast_to(ghost_x[side, c, 0, i : i + 1, :], (8, 128))
                second = jnp.broadcast_to(ghost_x[side, c, 1, i : i + 1, :], (8, 128))
                nodes.append(jnp.where(row2 < 4, first, second))
            u.append(jnp.stack(nodes))
        return [item.reshape(32, 128) for item in face_x(3 - a, f, cross(u, f))]

    def arrived_y(stage, a, b):
        part, slot = (0, a - 1) if a in (1, 2) else (1, a // 3)
        side = b // 3
        f = []
        for c in range(3):
            got = recv_y[stage, side, part, c, 16 * slot : 16 * (slot + 1), :]
            got = got.reshape(2, 8, 128)
            back = turn(got, 4, 0)
            if b == 0:
                full = jnp.where(row3 < 4, jnp.concatenate([got, back], axis=0), 0.0)
            else:
                full = jnp.where(row3 >= 4, jnp.concatenate([back, got], axis=0), 0.0)
            f.append(full)
        if stage == 0:
            u = []
            for c in range(3):
                low = 4 - 4 * side
                nodes = [
                    jnp.broadcast_to(ghost_y[side, c, a, i : i + 1, :], (8, 128))
                    for i in range(low, low + 4)
                ]
                u.append(jnp.stack(nodes))
            f = face_y(3 - b, f, cross(u, f))
        return [item.reshape(32, 128) for item in f]

    def emit_block(a, b):
        j = 4 * a + b
        for k in range(krylov):
            for c in range(3):
                out_ref[k, c, 8 * j : 8 * (j + 1), :] = state[
                    c, pl.ds(32 * j + k, 8, stride=4), :
                ]

    def add_block(target, a, b, found, scale):
        at = block(a, b)
        for c in range(3):
            target[c, at, :] = target[c, at, :] + (scale * PENALTY) * found[c]

    def rims(target, fresh, stage, scale, onward):
        for a in (0, 3):
            halo_wait(stage, 0, a // 3, 0)
            if stage == 0:
                ghost_wait(0, a // 3)
            for b in (1, 2):
                add_block(target, a, b, arrived_x(stage, a, b), scale)
                if onward:
                    f, e = cross_block(target, fresh, a, b)
                    pack_x(stage + 1, a, b, face_x(a, f, e))
                else:
                    emit_block(a, b)
            if onward:
                halo_start(stage + 1, 0, 1 - a // 3, 0)
        if stage == 0:
            for side in range(2):
                ghost_wait(1, side)
        for axis in range(2):
            for side in range(2):
                halo_wait(stage, axis, side, 1)
        for a in (0, 3):
            for b in (0, 3):
                fx = arrived_x(stage, a, b)
                fy = arrived_y(stage, a, b)
                add_block(target, a, b, [fx[c] + fy[c] for c in range(3)], scale)
                if onward:
                    f, e = cross_block(target, fresh, a, b)
                    pack_x(stage + 1, a, b, face_x(a, f, e))
                    pack_y(stage + 1, a, b, face_y(b, f, e))
                else:
                    emit_block(a, b)
            if onward:
                halo_start(stage + 1, 0, 1 - a // 3, 1)
        if onward:
            for side in range(2):
                halo_start(stage + 1, 1, side, 1)
        for b in (0, 3):
            halo_wait(stage, 1, b // 3, 0)
            for a in (1, 2):
                add_block(target, a, b, arrived_y(stage, a, b), scale)
                if onward:
                    f, e = cross_block(target, fresh, a, b)
                    pack_y(stage + 1, a, b, face_y(b, f, e))
                else:
                    emit_block(a, b)
            if onward:
                halo_start(stage + 1, 1, 1 - b // 3, 0)

    def first_faces():
        for a in range(4):
            for b in range(4):
                f = [state[c, block(a, b), :].reshape(4, 8, 128) for c in range(3)]
                if a in (0, 3):
                    pack_x(0, a, b, f)
                if b in (0, 3):
                    pack_y(0, a, b, f)
        for axis in range(2):
            for side in range(2):
                for part in range(2):
                    halo_start(0, axis, side, part)

    def inner(field, fresh):
        for a in (1, 2):
            for b in (1, 2):
                cross_block(field, fresh, a, b)

    def volume(field, a):
        b = [load(field, c, a) for c in range(3)]
        e = [load(elec, c, a) for c in range(3)]
        r = [
            d2(e[2]) - d3(e[1]),
            d3(e[0]) - combine(a, [load(elec, 2, q) for q in range(4)]),
            combine(a, [load(elec, 1, q) for q in range(4)]) - d2(e[0]),
        ]
        low2 = [b[0] - e[1], b[1] + e[0], b[2]]
        high2 = [b[0] + e[1], b[1] - e[0], b[2]]
        low1 = [b[0] + e[2], b[1], b[2] - e[0]]
        high1 = [b[0] - e[2], b[1], b[2] + e[0]]
        for c in range(3):
            from_below = jnp.where(lane > 0, turn(high2[c][:, 3:4], 1, 1), 0.0)
            from_above = jnp.where(lane < 127, turn(low2[c][:, 0:1], 127, 1), 0.0)
            gap = jnp.zeros((4, 2, 8, 128), jnp.float32)
            jump = jnp.concatenate(
                [from_below - b[c][:, 0:1], gap, from_above - b[c][:, 3:4]], axis=1
            )
            from_below = jnp.where(row >= 4, turn(high1[c][3:4], 4, 0), 0.0)
            from_above = jnp.where(row < 4, turn(low1[c][0:1], 4, 0), 0.0)
            gap = jnp.zeros((2, 4, 8, 128), jnp.float32)
            jump = jump + jnp.concatenate(
                [from_below - b[c][0:1], gap, from_above - b[c][3:4]], axis=0
            )
            if a in (0, 3):
                jump = jump - b[c]
            r[c] = r[c] + PENALTY * jump
        return b, r

    for axis, buffer in ((0, ghost_x), (1, ghost_y)):
        for side in range(2):

            @pl.when(jnp.logical_not(takes[axis][side]))
            def _():
                buffer[side] = jnp.zeros(buffer.shape[1:], jnp.float32)

    for axis, buffer in ((0, recv_x), (1, recv_y)):
        for side in range(2):

            @pl.when(jnp.logical_not(takes[axis][side]))
            def _():
                for stage in range(2 * phases):
                    for part in range(2):
                        for c in range(3):
                            buffer[stage, side, part, c] = jnp.zeros(buffer.shape[4:], jnp.float32)

    loads[0].wait()
    pack_phase(0)
    pl.semaphore_wait(barrier, devices - 1)
    send_phase(0)
    loads[phases].wait()

    for k in range(krylov):
        for c in range(3):
            for j in range(16):
                state[c, pl.ds(32 * j + k, 8, stride=4), :] = fields_ref[
                    k, c, 8 * j : 8 * (j + 1), :
                ]
    first_faces()
    for s in range(1, phases):
        loads[s].wait()
        pack_phase(s)
        send_phase(s)

    finish_phase(0)
    ghost_start()
    for s in range(phases):
        stage = 2 * s
        last = s + 1 == phases
        if s == 0:
            for a in (0, 3):
                for b in range(4):
                    cross_block(state, 0, a, b)
            for a in (1, 2):
                for b in (0, 3):
                    cross_block(state, 0, a, b)
        inner(state, s)
        for a in range(4):
            b, r = volume(state, a)
            for c in range(3):
                store(middle, c, a, b[c] + STEP_SIZE * r[c])
        rims(middle, None, stage, STEP_SIZE, True)
        inner(middle, None)
        for a in range(4):
            b, r = volume(middle, a)
            for c in range(3):
                mean = 0.5 * (load(state, c, a) + b[c])
                store(state, c, a, mean + (0.5 * STEP_SIZE) * r[c])
        if last:
            for a in (1, 2):
                for b in (1, 2):
                    emit_block(a, b)
        else:
            finish_phase(s + 1)
        rims(state, s + 1, stage + 1, 0.5 * STEP_SIZE, not last)

    for s in range(phases):
        drain_phase(s)
    ghost_drain()
    for stage in range(2 * phases):
        halo_drain(stage)


def shards(count_x, count_y, fields, velocity):
    krylov, comps, nodes, elem_x, elem_y, depth = fields.shape
    phases, _, _, slab, wide_x, wide_y = velocity.shape
    devices = count_x * count_y
    stages = 2 * phases
    f32 = jnp.float32
    rows = nodes * elem_x * elem_y
    lines = krylov * rows
    body = functools.partial(kernel, count_x, count_y)
    vmem = pl.BlockSpec(memory_space=pltpu.VMEM)
    out = pl.pallas_call(
        body,
        out_shape=jax.ShapeDtypeStruct((krylov, comps, rows, depth), f32),
        in_specs=[pl.BlockSpec(memory_space=pl.ANY)] * 2,
        out_specs=vmem,
        scratch_shapes=[
            pltpu.VMEM((krylov, comps, rows, depth), f32),
            pltpu.VMEM((phases, comps, slab, wide_x, wide_y, nodes), f32),
            pltpu.VMEM((phases, devices, comps, slab, 128), f32),
            pltpu.VMEM((phases, devices, comps, slab, 128), f32),
            pltpu.VMEM((comps, depth, 128), f32),
            pltpu.VMEM((phases, comps, 2, 4, 16, depth), f32),
            pltpu.VMEM((comps, lines, depth), f32),
            pltpu.VMEM((comps, lines, depth), f32),
            pltpu.VMEM((comps, lines, depth), f32),
            pltpu.VMEM((comps, lines, depth), f32),
            pltpu.VMEM((stages, 2, 2, comps, 64, depth), f32),
            pltpu.VMEM((stages, 2, 2, comps, 64, depth), f32),
            pltpu.VMEM((stages, 2, 2, comps, 32, depth), f32),
            pltpu.VMEM((stages, 2, 2, comps, 32, depth), f32),
            pltpu.SemaphoreType.DMA((phases, devices)),
            pltpu.SemaphoreType.DMA((phases, devices)),
            pltpu.SemaphoreType.DMA((stages, 2, 2)),
            pltpu.SemaphoreType.DMA((stages, 2, 2)),
            pltpu.SemaphoreType.DMA((stages, 2, 2)),
            pltpu.SemaphoreType.DMA((stages, 2, 2)),
            pltpu.SemaphoreType.DMA((phases + 1,)),
            pltpu.VMEM((2, comps, 2, 16, depth), f32),
            pltpu.VMEM((2, comps, 4, 8, depth), f32),
            pltpu.SemaphoreType.DMA((2,)),
            pltpu.SemaphoreType.DMA((2,)),
            pltpu.SemaphoreType.DMA((2,)),
            pltpu.SemaphoreType.DMA((2,)),
        ],
        compiler_params=pltpu.CompilerParams(
            collective_id=0, has_side_effects=True, vmem_limit_bytes=54016 * 1024
        ),
    )(
        fields.reshape(krylov, comps, rows, depth),
        jnp.transpose(velocity, (0, 1, 3, 4, 5, 2)),
    )
    return out.reshape(fields.shape)


def solution(mesh):
    return jax.shard_map(
        functools.partial(shards, mesh.shape["gx"], mesh.shape["gy"]),
        mesh=mesh,
        in_specs=(
            P(None, None, None, "gx", "gy", None),
            P(None, None, None, ("gx", "gy"), None, None),
        ),
        out_specs=P(None, None, None, "gx", "gy", None),
        check_vma=False,
    )
```
